256 devices in a mesh: rep: 32 (over z, x), row: 4 (over y), col: 2 (over core).
Axes of the slice: x: 4, y: 4, z: 8, core: 2. Of those that a mesh axis runs over, the one named last changes fastest.
Arguments:
- tokens: bfloat16 [1024, 5120], P(('rep', 'col'), 'row'), may hold values from -6 to 6
- w_in: bfloat16 [5120, 10240], P('row', ('rep', 'col')), may hold values from -0.078125 to 0.078125
- w_out: bfloat16 [10240, 5120], P(('rep', 'col'), 'row'), may hold values from -0.0625 to 0.0625
- cotangent: bfloat16 [1024, 5120], P(('rep', 'col'), 'row'), may hold values from -3 to 3
Outputs:
- output: bfloat16 [1024, 5120], P(('rep', 'col'), 'row')
- input_grad: bfloat16 [1024, 5120], P(('rep', 'col'), 'row')
- grad_in: float32 [5120, 10240], P('row', ('rep', 'col'))
- grad_out: float32 [10240, 5120], P(('rep', 'col'), 'row')
The draws below stay inside these ranges and needn't reach their ends.
All inputs are finite; a program needn't handle non-finite values.
Results may differ from the reference program's by a relative error of at most 0.0049.
Values may be sent and summed in bfloat16 or wider, within the bound.
No kernel may reach another device: no remote copies, remote signals or barrier semaphores. Data moves between devices by JAX's collectives and lax.ppermute only.
A program may use at most 64 MiB of HBM per device.

```python
import jax
import jax.numpy as jnp

D = 5120
FF = 10240
ALL = 1024


def levels(rng, shape, pieces, least, high):
    factor_of = 1.0
    for dim, parts in pieces:
        heights = jax.random.uniform(jax.random.fold_in(jax.random.fold_in(rng, 6), dim), (parts,), jnp.float32, least / len(pieces), high / len(pieces))
        factor_of = factor_of * jnp.repeat(jnp.exp(heights), shape[dim] // parts).reshape((-1,) + (1,) * (len(shape) - 1 - dim))
    return factor_of


def gaussian(own_key, dims, scale, reach, pieces=(), kind=jnp.bfloat16):
    drawn = scale * jax.random.normal(own_key, dims, jnp.float32)
    if pieces:
        drawn = drawn * levels(own_key, dims, pieces, -0.22, 0.18)
    return jnp.clip(drawn, -reach, reach).astype(kind)


def setup_inputs(seed: int = 0) -> dict:
    splits = jax.random.split(jax.random.key(seed), 5)
    tokens = gaussian(splits[0], (ALL, D), 1.0, 6.0, ((0, 64), (1, 4)))
    w_in = gaussian(splits[1], (D, FF), D ** -0.5, 0.078125, ((0, 4), (1, 64)))
    w_out = gaussian(splits[2], (FF, D), FF ** -0.5, 0.0625, ((0, 64), (1, 4)))
    cotangent = gaussian(splits[3], (ALL, D), 0.5, 3.0, ((0, 64), (1, 4)))
    return dict(tokens=tokens, w_in=w_in, w_out=w_out, cotangent=cotangent)


def smooth_gate(value):
    return 0.5 * value * (1.0 + jax.scipy.special.erf(value * 0.7071067811865476))


def smooth_slope(value):
    cumul = 0.5 * (1.0 + jax.scipy.special.erf(value * 0.7071067811865476))
    return cumul + value * jnp.exp(-0.5 * value * value) * 0.3989422804014327


def reference(tokens, w_in, w_out, cotangent):
    pre = jnp.dot(tokens, w_in, preferred_element_type=jnp.float32)
    act = smooth_gate(pre).astype(jnp.bfloat16)
    output = jnp.dot(act, w_out, preferred_element_type=jnp.float32).astype(jnp.bfloat16)
    grad_act = jnp.dot(cotangent, w_out.T, preferred_element_type=jnp.float32)
    grad_pre = (grad_act * smooth_slope(pre)).astype(jnp.bfloat16)
    input_grad = jnp.dot(grad_pre, w_in.T, preferred_element_type=jnp.float32).astype(jnp.bfloat16)
    grad_in = jnp.dot(tokens.T, grad_pre, preferred_element_type=jnp.float32)
    grad_out = jnp.dot(act.T, cotangent, preferred_element_type=jnp.float32)
    return output, input_grad, grad_in, grad_out
```

```python
import jax
import jax.numpy as jnp
from jax import lax
from jax.sharding import Mesh, PartitionSpec as P

BF = jnp.bfloat16
F32 = jnp.float32
SIZE = {"z": 8, "x": 4, "row": 4, "col": 2}


def smooth_gate(value):
    return 0.5 * value * (1.0 + jax.scipy.special.erf(value * 0.7071067811865476))


def smooth_slope(value):
    cumul = 0.5 * (1.0 + jax.scipy.special.erf(value * 0.7071067811865476))
    return cumul + value * jnp.exp(-0.5 * value * value) * 0.3989422804014327


def send(value, axis, shift):
    size = SIZE[axis]
    return lax.ppermute(value, axis, [(i, (i + shift) % size) for i in range(size)])


def ring_gather(value, axis):
    size = SIZE[axis]
    half = size // 2
    out = [None] * size
    out[0] = up = down = value
    for step in range(1, half):
        up, down = send(up, axis, -1), send(down, axis, 1)
        out[step], out[size - step] = up, down
    cut = value.shape[0] // 2
    out[half] = jnp.concatenate(
        [send(up[:cut], axis, -1), send(down[cut:], axis, 1)], 0
    )
    return out


def ring_sum(blocks, axis):
    size = SIZE[axis]
    half = size // 2
    up = send(blocks[half].astype(BF), axis, 1).astype(F32)
    down = None
    for k in range(half - 1, 0, -1):
        up = send((up + blocks[k]).astype(BF), axis, 1).astype(F32)
        own = blocks[size - k]
        down = own if down is None else down + own
        down = send(down.astype(BF), axis, -1).astype(F32)
    return blocks[0] + up + down


def row_sum(parts, me):
    total = lax.dynamic_index_in_dim(parts, me, 0, False)
    for k in range(1, 4):
        part = lax.dynamic_index_in_dim(parts, (me + k) % 4, 0, False)
        total = total + send(part, "row", k)
    return total


def row_gather(value, me):
    rel = [value] + [send(value, "row", -k) for k in range(1, 4)]
    twice = jnp.stack(rel + rel)
    return lax.dynamic_slice_in_dim(twice, (4 - me) % 4, 4, 0)


def scatter(own, other, x_first):
    d = own.shape[-1]
    total = own + send(other, "col", 1).astype(F32)
    total = total.reshape(8, 4, 16, d)
    if x_first:
        total = ring_sum([total[:, k] for k in range(4)], "x")
        total = ring_sum([total[k] for k in range(8)], "z")
    else:
        total = ring_sum([total[k] for k in range(8)], "z")
        total = ring_sum([total[k] for k in range(4)], "x")
    return total.astype(BF)


def on_device(tokens, w_in, w_out, cotangent):
    me = lax.axis_index("row")
    t, d = tokens.shape
    h = w_in.shape[1]
    both = jnp.concatenate([tokens, cotangent], 0)
    plane = jnp.stack(ring_gather(jnp.concatenate(ring_gather(both, "x"), 0), "z"))
    plane = plane.reshape(8, 4, 2, t, d)
    tok_half = plane[:, :, 0].reshape(-1, d)
    cot_half = plane[:, :, 1].reshape(-1, d)
    tok = jnp.concatenate([tok_half, send(tok_half, "col", 1)], 0).reshape(4, 256, d)
    cot = jnp.concatenate([cot_half, send(cot_half, "col", 1)], 0).reshape(4, 256, d)

    pre_part = jnp.einsum("dh,qtd->qht", w_in, tok, preferred_element_type=F32)
    pre = row_sum(pre_part, me)
    act = row_gather(smooth_gate(pre).astype(BF), me)
    ga_part = jnp.einsum("hd,qtd->qht", w_out, cot, preferred_element_type=F32)
    grad_act = row_sum(ga_part, me)
    grad = row_gather((grad_act * smooth_slope(pre)).astype(BF), me)

    out_own = jnp.einsum("qht,hd->qtd", act[:2], w_out, preferred_element_type=F32)
    out_other = jnp.einsum("qht,hd->qtd", act[2:], w_out, preferred_element_type=F32)
    back_own = jnp.einsum("qht,dh->qtd", grad[:2], w_in, preferred_element_type=F32)
    back_other = jnp.einsum("qht,dh->qtd", grad[2:], w_in, preferred_element_type=F32)
    output = scatter(out_own.reshape(-1, d), out_other.astype(BF).reshape(-1, d), True)
    input_grad = scatter(
        back_own.reshape(-1, d), back_other.astype(BF).reshape(-1, d), False
    )
    grad_in = jnp.einsum("qtd,qht->dh", tok, grad, preferred_element_type=F32)
    grad_out = jnp.einsum("qht,qtd->hd", act, cot, preferred_element_type=F32)
    return (output, input_grad, grad_in, grad_out)


def solution(mesh):
    mesh = Mesh(mesh.devices.reshape(8, 4, 4, 2), ("z", "x", "row", "col"))
    whole = ("z", "x", "col")
    placed = (P(whole, "row"), P("row", whole), P(whole, "row"), P(whole, "row"))
    return jax.shard_map(
        on_device,
        mesh=mesh,
        in_specs=placed,
        out_specs=(P(whole, "row"), P(whole, "row"), P("row", whole), P(whole, "row")),
        check_vma=False,
    )
```

```python
import jax
import jax.numpy as jnp
from jax import lax
from jax.experimental import pallas as pl
from jax.experimental.pallas import tpu as pltpu
from jax.sharding import Mesh, PartitionSpec as P

BF = jnp.bfloat16
F32 = jnp.float32
SIZE = {"z": 8, "x": 4, "row": 4, "col": 2}
ORDER = (0, 1, 7, 2, 6, 3, 5, 4)
HEAD = 5


def smooth_gate(value):
    return 0.5 * value * (1.0 + jax.scipy.special.erf(value * 0.7071067811865476))


def smooth_slope(value):
    cumul = 0.5 * (1.0 + jax.scipy.special.erf(value * 0.7071067811865476))
    return cumul + value * jnp.exp(-0.5 * value * value) * 0.3989422804014327


def send(value, axis, shift):
    size = SIZE[axis]
    return lax.ppermute(value, axis, [(i, (i + shift) % size) for i in range(size)])


def after(value, other):
    return lax.optimization_barrier((value, other))[0]


def vmem(n):
    return [pl.BlockSpec(memory_space=pltpu.VMEM)] * n


def call(body, outs, n_in, flops, scratch=()):
    nbytes = 1 << 20
    return pl.pallas_call(
        body,
        out_shape=outs,
        in_specs=[pl.BlockSpec(memory_space=pltpu.SMEM)] + vmem(n_in),
        out_specs=vmem(len(outs)),
        scratch_shapes=list(scratch),
        compiler_params=pltpu.CompilerParams(vmem_limit_bytes=40 << 20),
        cost_estimate=pl.CostEstimate(
            flops=flops, bytes_accessed=nbytes, transcendentals=0
        ),
    )


def last(a, b):
    return lax.dot_general(a, b, (((1,), (1,)), ((), ())), preferred_element_type=F32)


def first(a, b):
    return lax.dot_general(a, b, (((0,), (0,)), ((), ())), preferred_element_type=F32)


def up_kernel(me, own_a, own_b, oth_a, oth_b, w, full, *parts):
    q = full.shape[1]
    rest = own_a.shape[0] - q
    full[0] = own_a[:q]
    full[1, :rest] = own_a[q:]
    full[1, rest:] = own_b[...]
    full[2] = oth_a[:q]
    full[3, :rest] = oth_a[q:]
    full[3, rest:] = oth_b[...]
    for k in range(4):
        parts[k][...] = last(w[...], full[(me[0] + k) % 4])


def down_kernel(me, *refs):
    blocks, (w, own, oth_a, oth_b, full) = refs[:4], refs[4:]
    for k in range(4):
        full[(me[0] + k) % 4] = blocks[k][...]
    q = full.shape[2]
    rest = oth_a.shape[0] - q
    for a in (3, 2):
        value = first(full[a], w[...]).astype(BF)
        if a == 2:
            oth_a[:q] = value
        else:
            oth_a[q:] = value[:rest]
            oth_b[...] = value[rest:]
    for a in (0, 1):
        own[a * q : (a + 1) * q] = first(full[a], w[...])


def grad_kernel(me, act, value, out):
    del me
    total = jnp.dot(act[0], value[0], preferred_element_type=F32)
    for a in range(1, 4):
        total += jnp.dot(act[a], value[a], preferred_element_type=F32)
    out[...] = total


def gather(tokens, cotangent):
    t, d = tokens.shape
    both = jnp.concatenate([tokens, cotangent], 0)
    xs = [both] + [send(both, "x", -k) for k in range(1, 4)]
    streams = []
    for s in range(2):
        base = jnp.concatenate([b[s * t : (s + 1) * t] for b in xs], 0)
        streams.append({0: base})
    up = [streams[0][0], streams[1][0]]
    down = list(up)
    previous = None
    heads = [None, None]
    for step in range(1, 5):
        for s in range(2):
            if previous is not None:
                up[s], down[s] = after((up[s], down[s]), previous)
            previous = (up[s], down[s])
            if step < 4 or s == 0:
                up[s] = send(up[s], "z", -1)
                streams[s][step] = up[s]
            if step < 4 or s == 1:
                down[s] = send(down[s], "z", 1)
                streams[s][8 - step] = down[s]
    out = []
    for s in range(2):
        head = jnp.concatenate([streams[s][k] for k in ORDER[:HEAD]], 0)
        tail = jnp.concatenate([streams[s][k] for k in ORDER[HEAD:]], 0)
        out.append((head, tail, send(head, "col", 1), send(tail, "col", 1)))
    return out


def row_sum(parts):
    total = parts[0]
    for k in range(1, 4):
        total = total + send(parts[k], "row", k)
    return total


def row_gather(value):
    return [value] + [send(value, "row", -k) for k in range(1, 4)]


def scatter(streams):
    pieces = []
    for own, oth_a, oth_b in streams:
        tail = send(oth_b, "col", 1)
        head = send(oth_a, "col", 1)
        t = oth_b.shape[0] // (8 - HEAD)
        mine = {}
        for i, k in enumerate(ORDER):
            got = head[i * t : (i + 1) * t] if i < HEAD else tail[(i - HEAD) * t : (i - HEAD + 1) * t]
            mine[k] = own[i * t : (i + 1) * t] + got.astype(F32)
        pieces.append(mine)
    up, down = [None, None], [None, None]
    for k in (4, 3, 2, 1):
        for s in range(2):
            if k < 4 or s == 0:
                value = pieces[s][k] if up[s] is None else up[s] + pieces[s][k]
                up[s] = send(value.astype(BF), "z", 1).astype(F32)
            if k < 4 or s == 1:
                value = pieces[s][8 - k]
                value = value if down[s] is None else down[s] + value
                down[s] = send(value.astype(BF), "z", -1).astype(F32)
    sums = []
    for s in range(2):
        total = pieces[s][0] + up[s] + down[s]
        sums.append(total.reshape(4, total.shape[0] // 4, -1))
    total = jnp.concatenate([sums[0][0], sums[1][0]], 0)
    for k in range(1, 4):
        value = jnp.concatenate([sums[0][k], sums[1][k]], 0)
        total = total + send(value.astype(BF), "x", k).astype(F32)
    total = total.astype(BF)
    n = total.shape[0] // 2
    return total[:n], total[n:]


def on_device(tokens, w_in, w_out, cotangent):
    me = lax.axis_index("row").astype(jnp.int32).reshape(1)
    d, h = w_in.shape
    w_in_t = w_in.T
    tok, cot = gather(tokens, cotangent)
    t = (tok[0].shape[0] + tok[1].shape[0]) // 2
    part = jax.ShapeDtypeStruct((h, t), F32)
    full = jax.ShapeDtypeStruct((4, t, d), BF)
    flops = 8 * t * d * h
    tok_full, *pre_parts = call(up_kernel, [full] + [part] * 4, 5, flops)(me, *tok, w_in_t)
    cot_full, *ga_parts = call(up_kernel, [full] + [part] * 4, 5, flops)(me, *cot, w_out)
    pre = row_sum(pre_parts)
    acts = row_gather(smooth_gate(pre).astype(BF))
    grad_act = row_sum(ga_parts)
    grads = row_gather((grad_act * smooth_slope(pre)).astype(BF))

    outs = [
        jax.ShapeDtypeStruct((2 * t, d), F32),
        jax.ShapeDtypeStruct(tok[0].shape, BF),
        jax.ShapeDtypeStruct(tok[1].shape, BF),
        jax.ShapeDtypeStruct((4, h, t), BF),
    ]
    out_own, out_a, out_b, act = call(down_kernel, outs, 5, flops)(me, *acts, w_out)
    back_own, back_a, back_b, grad = call(down_kernel, outs, 5, flops)(me, *grads, w_in_t)
    output, input_grad = scatter([(out_own, out_a, out_b), (back_own, back_a, back_b)])
    weight = [jax.ShapeDtypeStruct((h, d), F32)]
    (grad_out,) = call(grad_kernel, weight, 2, flops)(me, act, cot_full)
    (grad_in_t,) = call(grad_kernel, weight, 2, flops)(me, grad, tok_full)
    return (output, input_grad, grad_in_t.T, grad_out)


def solution(mesh):
    mesh = Mesh(mesh.devices.reshape(8, 4, 4, 2), ("z", "x", "row", "col"))
    whole = ("z", "x", "col")
    placed = (P(whole, "row"), P("row", whole), P(whole, "row"), P(whole, "row"))
    return jax.shard_map(
        on_device,
        mesh=mesh,
        in_specs=placed,
        out_specs=(P(whole, "row"), P(whole, "row"), P("row", whole), P(whole, "row")),
        check_vma=False,
    )
```

```python
import jax
import jax.numpy as jnp
from jax import lax
from jax.experimental import pallas as pl
from jax.experimental.pallas import tpu as pltpu
from jax.sharding import Mesh, PartitionSpec as P

BF = jnp.bfloat16
F32 = jnp.float32
SIZE = {"z": 8, "x": 4, "row": 4, "col": 2}
ORDER = (0, 1, 7, 2, 6, 3, 5, 4)
XORDER = (0, 1, 3, 2)


def smooth_gate(value):
    return 0.5 * value * (1.0 + lax.erf(value * 0.7071067811865476))


def smooth_slope(value):
    cumul = 0.5 * (1.0 + lax.erf(value * 0.7071067811865476))
    return cumul + value * jnp.exp(-0.5 * value * value) * 0.3989422804014327


class Issue:
    def __init__(self):
        self.previous = None

    def after(self, value):
        if self.previous is not None:
            value = lax.optimization_barrier((value, self.previous))[0]
        self.previous = value
        return value

    def send(self, value, axis, shift):
        size = SIZE[axis]
        pairs = [(i, (i + shift) % size) for i in range(size)]
        return lax.ppermute(self.after(value), axis, pairs)

    def call(self, body, outs, args, flops=1 << 20, scratch=()):
        specs = [pl.BlockSpec(memory_space=pltpu.SMEM)]
        specs += [pl.BlockSpec(memory_space=pltpu.VMEM)] * (len(args) - 1)
        args = list(args)
        args[1] = self.after(args[1])
        kernel = pl.pallas_call(
            body,
            out_shape=outs,
            in_specs=specs,
            out_specs=[pl.BlockSpec(memory_space=pltpu.VMEM)] * len(outs),
            scratch_shapes=list(scratch),
            compiler_params=pltpu.CompilerParams(vmem_limit_bytes=40 << 20),
            cost_estimate=pl.CostEstimate(
                flops=flops, bytes_accessed=1 << 20, transcendentals=0
            ),
        )
        return list(kernel(*args))


def cat(values):
    return jnp.concatenate(values, 0)


def last(a, b):
    return lax.dot_general(a, b, (((1,), (1,)), ((), ())), preferred_element_type=F32)


def first(a, b):
    return lax.dot_general(a, b, (((0,), (0,)), ((), ())), preferred_element_type=F32)


def up_a_kernel(me, q0, q1, q2, q3, w, *refs):
    parts, whole = refs[:4], refs[4]
    for a, quarter in enumerate((q0, q1, q2, q3)):
        whole[a] = last(w[...], quarter[...])
    for k in range(4):
        parts[k][...] = whole[(me[0] + k) % 4]


def up_b_kernel(me, own, own2, oth, oth2, w, full, *parts):
    for half, (near, far) in enumerate(((own, own2), (oth, oth2))):
        for slot, z in enumerate(ORDER):
            for i, x in enumerate(XORDER):
                ref, base = (near, i * 128) if i < 3 else (far, 0)
                row = (slot % 4) * 64 + x * 16
                full[half * 2 + slot // 4, row : row + 16] = ref[
                    base + z * 16 : base + z * 16 + 16
                ]
    for k in range(4):
        parts[k][...] = last(w[...], full[(me[0] + k) % 4])


def act_kernel(me, p0, p1, p2, p3, act, slope):
    del me
    pre = p0[...] + p1[...] + p2[...] + p3[...]
    act[...] = smooth_gate(pre).astype(BF)
    slope[...] = smooth_slope(pre)


def slope_kernel(me, p0, p1, p2, p3, slope, grad):
    del me
    value = p0[...] + p1[...] + p2[...] + p3[...]
    grad[...] = (value * slope[...]).astype(BF)


def down_a_kernel(me, b0, b1, b2, b3, w, own, oth_a, oth_b, full):
    for k, block in enumerate((b0, b1, b2, b3)):
        full[(me[0] + k) % 4] = block[...]
    oth_b[...] = first(full[3], w[...]).astype(BF)
    oth_a[...] = first(full[2], w[...]).astype(BF)
    for a in (0, 1):
        own[a * 256 : a * 256 + 256] = first(full[a], w[...])


def down_b_kernel(me, b0, b1, b2, b3, w, own, oth, oth2, full):
    for k, block in enumerate((b0, b1, b2, b3)):
        full[(me[0] + k) % 4] = block[...]
    for a in (2, 3, 0, 1):
        value = first(full[a], w[...])
        for j in range(4):
            z = ORDER[(a % 2) * 4 + j]
            for i, x in enumerate(XORDER):
                block = value[j * 64 + x * 16 : j * 64 + x * 16 + 16]
                row = i * 128 + z * 16
                if a < 2:
                    own[row : row + 16] = block
                elif i < 3:
                    oth[row : row + 16] = block.astype(BF)
                else:
                    oth2[z * 16 : z * 16 + 16] = block.astype(BF)


def grad_a_kernel(me, act, value, out):
    del me
    total = jnp.dot(act[0], value[0], preferred_element_type=F32)
    for a in range(1, 4):
        total += jnp.dot(act[a], value[a], preferred_element_type=F32)
    out[...] = total


def grad_b_kernel(me, act, q0, q1, q2, q3, out):
    del me
    total = jnp.dot(act[0], q0[...], preferred_element_type=F32)
    for a, quarter in ((1, q1), (2, q2), (3, q3)):
        total += jnp.dot(act[a], quarter[...], preferred_element_type=F32)
    out[...] = total


def on_device(tokens, w_in, w_out, cotangent):
    me = lax.axis_index("row").astype(jnp.int32).reshape(1)
    d, h = w_in.shape
    w_in_t = w_in.T
    go = Issue()
    shape = jax.ShapeDtypeStruct
    flops = 2 * 1024 * d * h

    tx = {k: go.send(tokens, "x", -k) for k in (1, 3, 2)}
    cz = {k: go.send(cotangent, "z", -k) for k in (1, 7, 2)}
    tz = {0: cat([tokens, tx[1], tx[2], tx[3]])}
    tz[1], tz[7] = go.send(tz[0], "z", -1), go.send(tz[0], "z", 1)
    cz.update({k: go.send(cotangent, "z", -k) for k in (6, 3, 5, 4)})
    tz[2], tz[6] = go.send(tz[1], "z", -1), go.send(tz[7], "z", 1)
    cz[0] = cotangent
    cx = {0: cat([cz[k] for k in range(8)])}
    cx[1], cx[3] = go.send(cx[0], "x", -1), go.send(cx[0], "x", 1)
    tz[3], tz[5] = go.send(tz[2], "z", -1), go.send(tz[6], "z", 1)
    own_a = cat([tz[k] for k in ORDER[:4]])
    oth_a = go.send(own_a, "col", 1)
    tz[4] = go.send(tz[3], "z", -1)
    c2 = go.send(cx[1][:64], "x", -1), go.send(cx[3][64:], "x", 1)
    own_b = cat([tz[k] for k in ORDER[4:]])
    oth_b = go.send(own_b, "col", 1)
    c_own = cat([cx[k] for k in XORDER[:3]])
    c_oth = go.send(c_own, "col", 1)
    quarters = [own_a, own_b, oth_a, oth_b]

    part = shape((h, 256), F32)
    half = shape((h, 256), BF)
    pre = go.call(
        up_a_kernel, [part] * 4, [me, *quarters, w_in_t], flops,
        [pltpu.VMEM((4, h, 256), F32)],
    )
    pre[1:] = [go.send(pre[k], "row", k) for k in (1, 2, 3)]
    c_own2 = cat(c2)
    c_oth2 = go.send(c_own2, "col", 1)
    cot, *gact = go.call(
        up_b_kernel, [shape((4, 256, d), BF)] + [part] * 4,
        [me, c_own, c_own2, c_oth, c_oth2, w_out], flops,
    )
    gact[1:] = [go.send(gact[k], "row", k) for k in (1, 2, 3)]
    act, slope = go.call(act_kernel, [half, part], [me, *pre])
    acts = [act] + [go.send(act, "row", -k) for k in (1, 2, 3)]
    (grad,) = go.call(slope_kernel, [half], [me, *gact, slope])
    grads = [grad] + [go.send(grad, "row", -k) for k in (1, 2, 3)]

    full = shape((4, h, 256), BF)
    o_own, o_a, o_b, act = go.call(
        down_a_kernel,
        [shape((512, d), F32), shape((256, d), BF), shape((256, d), BF), full],
        [me, *acts, w_out], flops,
    )
    o_b = go.send(o_b, "col", 1)
    o_a = go.send(o_a, "col", 1)
    oz = {}
    for i, k in enumerate(ORDER):
        got = o_a if i < 4 else o_b
        oz[k] = o_own[i * 64 : i * 64 + 64] + got[i % 4 * 64 : i % 4 * 64 + 64].astype(F32)
    up = go.send(oz[4].astype(BF), "z", 1)
    b_own, b_oth, b_oth2, grad = go.call(
        down_b_kernel,
        [shape((512, d), F32), shape((384, d), BF), shape((128, d), BF), full],
        [me, *grads, w_in_t], flops,
    )
    b_oth2 = go.send(b_oth2, "col", 1)
    up = go.send((up.astype(F32) + oz[3]).astype(BF), "z", 1)
    down = go.send(oz[5].astype(BF), "z", -1)
    b_oth = go.send(b_oth, "col", 1)
    bx = {}
    for i, x in enumerate(XORDER):
        got = b_oth[i * 128 : i * 128 + 128] if i < 3 else b_oth2
        bx[x] = b_own[i * 128 : i * 128 + 128] + got.astype(F32)
    b_up = go.send(bx[2][:64].astype(BF), "x", 1)
    b_down = go.send(bx[2][64:].astype(BF), "x", -1)
    up = go.send((up.astype(F32) + oz[2]).astype(BF), "z", 1)
    down = go.send((down.astype(F32) + oz[6]).astype(BF), "z", -1)
    b_up = cat([b_up.astype(F32) + bx[1][:64], bx[1][64:]])
    b_down = cat([bx[3][:64], b_down.astype(F32) + bx[3][64:]])
    b_up = go.send(b_up.astype(BF), "x", 1)
    b_down = go.send(b_down.astype(BF), "x", -1)
    weight = [shape((h, d), F32)]
    (grad_out,) = go.call(grad_a_kernel, weight, [me, act, cot], flops)
    up = go.send((up.astype(F32) + oz[1]).astype(BF), "z", 1)
    down = go.send((down.astype(F32) + oz[7]).astype(BF), "z", -1)
    (grad_in_t,) = go.call(grad_b_kernel, weight, [me, grad, *quarters], flops)
    bz = (bx[0] + b_up.astype(F32) + b_down.astype(F32)).reshape(8, 16, d)
    ox = (oz[0] + up.astype(F32) + down.astype(F32)).reshape(4, 16, d)
    input_grad = bz[0]
    for k in (4, 3, 5, 2, 6, 1, 7):
        input_grad += go.send(bz[k].astype(BF), "z", k).astype(F32)
    output = ox[0]
    for k in (2, 1, 3):
        output += go.send(ox[k].astype(BF), "x", k).astype(F32)
    return (output.astype(BF), input_grad.astype(BF), grad_in_t.T, grad_out)


def solution(mesh):
    mesh = Mesh(mesh.devices.reshape(8, 4, 4, 2), ("z", "x", "row", "col"))
    whole = ("z", "x", "col")
    placed = (P(whole, "row"), P("row", whole), P(whole, "row"), P(whole, "row"))
    return jax.shard_map(
        on_device,
        mesh=mesh,
        in_specs=placed,
        out_specs=(P(whole, "row"), P(whole, "row"), P("row", whole), P(whole, "row")),
        check_vma=False,
    )
```

```python
import jax
import jax.numpy as jnp
from jax import lax
from jax.experimental import pallas as pl
from jax.experimental.pallas import tpu as pltpu
from jax.sharding import Mesh, PartitionSpec as P

BF = jnp.bfloat16
F32 = jnp.float32
SIZE = {"z": 8, "x": 4, "row": 4, "col": 2}
ORDER = (0, 1, 7, 2, 6, 3, 5, 4)


def smooth_gate(value):
    return 0.5 * value * (1.0 + lax.erf(value * 0.7071067811865476))


def smooth_slope(value):
    cumul = 0.5 * (1.0 + lax.erf(value * 0.7071067811865476))
    return cumul + value * jnp.exp(-0.5 * value * value) * 0.3989422804014327


def send(value, axis, shift):
    size = SIZE[axis]
    return lax.ppermute(value, axis, [(i, (i + shift) % size) for i in range(size)])


def swap_pair(value):
    return lax.ppermute(value, "x", [(i, i ^ 1) for i in range(4)])


def after(value, other):
    return lax.optimization_barrier((value, other))[0]


def call(body, outs, args, flops=1 << 20, scratch=()):
    specs = [pl.BlockSpec(memory_space=pltpu.SMEM)]
    specs += [pl.BlockSpec(memory_space=pltpu.VMEM)] * (len(args) - 1)
    kernel = pl.pallas_call(
        body,
        out_shape=outs,
        in_specs=specs,
        out_specs=[pl.BlockSpec(memory_space=pltpu.VMEM)] * len(outs),
        scratch_shapes=list(scratch),
        compiler_params=pltpu.CompilerParams(vmem_limit_bytes=40 << 20),
        cost_estimate=pl.CostEstimate(
            flops=flops, bytes_accessed=1 << 20, transcendentals=0
        ),
    )
    return list(kernel(*args))


def cat(values):
    return jnp.concatenate(values, 0)


def dot(a, b, dim_a, dim_b):
    return lax.dot_general(
        a, b, (((dim_a,), (dim_b,)), ((), ())), preferred_element_type=F32
    )


def up_kernel(me, q0, q1, q2, q3, wi, wi2, wo, wo2, tok, cot, p0, p1, p2, p3, whole):
    h = wi.shape[0]
    for a, quarter in enumerate((q0, q1, q2, q3)):
        for j in range(4):
            row = a * 128 + j * 32
            tok[row : row + 32] = quarter[j * 64 : j * 64 + 32]
            cot[row : row + 32] = quarter[j * 64 + 32 : j * 64 + 64]
    for s, (weights, value) in enumerate((((wi, wi2), tok), ((wo, wo2), cot))):
        for i, w in enumerate(weights):
            total = dot(w[...], value[...], 1, 1)
            for a in range(4):
                whole[a, s, i * h : i * h + h] = total[:, a * 128 : a * 128 + 128]
    for k, part in enumerate((p0, p1, p2, p3)):
        part[...] = whole[(me[0] + k) % 4]


def act_kernel(me, p0, p1, p2, p3, out):
    del me
    pre = p0[0] + p1[0] + p2[0] + p3[0]
    grad_act = p0[1] + p1[1] + p2[1] + p3[1]
    out[0] = smooth_gate(pre).astype(BF)
    out[1] = (grad_act * smooth_slope(pre)).astype(BF)


def down_kernel(me, b0, b1, b2, b3, wi, wi2, wo, wo2, own, oth_a, oth_b, full):
    h = wi.shape[0]
    for k, block in enumerate((b0, b1, b2, b3)):
        lane = pl.multiple_of(((me[0] + k) % 4) * 128, 128)
        full[:, :, pl.ds(lane, 128)] = block[...]
    for s, (w, w2) in enumerate(((wo, wo2), (wi, wi2))):
        for half in (1, 0):
            value = dot(full[s, :h, half * 256 : half * 256 + 256], w[...], 0, 0)
            value += dot(full[s, h:, half * 256 : half * 256 + 256], w2[...], 0, 0)
            for j in range(8):
                piece = value[j * 32 : j * 32 + 32]
                row = j * 64 + s * 32
                if half == 0:
                    own[row : row + 32] = piece
                elif j < 4:
                    oth_a[row : row + 32] = piece.astype(BF)
                else:
                    oth_b[row - 256 : row - 224] = piece.astype(BF)


def pair_kernel(me, full, tok, cot, out):
    del me
    h = full.shape[1] // 2
    out[:h] = dot(full[0, h:], cot[...], 1, 0).astype(BF)
    out[h:] = dot(full[1, h:], tok[...], 1, 0).astype(BF)


def own_kernel(me, full, tok, cot, grad_out, grad_in):
    del me
    h = full.shape[1] // 2
    grad_out[...] = dot(full[0, :h], cot[...], 1, 0)
    grad_in[...] = dot(full[1, :h], tok[...], 1, 0)


def on_device(tokens, w_in, w_out, cotangent):
    me = lax.axis_index("row").astype(jnp.int32).reshape(1)
    d, h = w_in.shape
    shape = jax.ShapeDtypeStruct
    flops = 2 * 1024 * d * h

    far = send(cat([tokens, cotangent]), "x", 2)
    z = {0: cat([tokens, far[:16], cotangent, far[16:]])}
    z[1], z[7] = send(z[0], "z", -1), send(z[0], "z", 1)
    w_in_t = w_in.T
    w_in_2 = swap_pair(after(w_in_t, z[0]))
    w_out_2 = swap_pair(after(w_out, z[1]))
    z[2], z[6] = send(z[1], "z", -1), send(z[7], "z", 1)
    own_a = cat([z[k] for k in ORDER[:4]])
    z[3], z[5] = send(z[2], "z", -1), send(z[6], "z", 1)
    oth_a = send(own_a, "col", 1)
    z[4] = cat([send(z[3][:32], "z", -1), send(z[5][32:], "z", 1)])
    own_b = cat([z[k] for k in ORDER[4:]])
    oth_b = send(own_b, "col", 1)

    part = shape((2, 2 * h, 128), F32)
    tok, cot, *parts = call(
        up_kernel,
        [shape((512, d), BF)] * 2 + [part] * 4,
        [me, own_a, own_b, oth_a, oth_b, w_in_t, w_in_2, w_out, w_out_2],
        2 * flops,
        [pltpu.VMEM((4, 2, 2 * h, 128), F32)],
    )
    parts[1:] = [send(parts[k], "row", k) for k in (1, 2, 3)]
    (block,) = call(act_kernel, [shape((2, 2 * h, 128), BF)], [me, *parts])
    blocks = [block] + [send(block, "row", -k) for k in (1, 2, 3)]

    own, oth_a, oth_b, full = call(
        down_kernel,
        [shape((512, d), F32), shape((256, d), BF), shape((256, d), BF), shape((2, 2 * h, 512), BF)],
        [me, *blocks, w_in_t, w_in_2, w_out, w_out_2],
        2 * flops,
    )
    oth_b = send(oth_b, "col", 1)
    oth_a = send(oth_a, "col", 1)
    (pair,) = call(
        pair_kernel, [shape((2 * h, d), BF)], [me, after(full, oth_b), tok, cot], flops
    )
    piece = {}
    for i, k in enumerate(ORDER):
        got = oth_a if i < 4 else oth_b
        got = got[i % 4 * 64 : i % 4 * 64 + 64].astype(F32)
        piece[k] = own[i * 64 : i * 64 + 64] + got
    up = send(piece[4][:32].astype(BF), "z", 1).astype(F32)
    down = send(piece[4][32:].astype(BF), "z", -1).astype(F32)
    pair = swap_pair(pair)
    up = cat([up + piece[3][:32], piece[3][32:]])
    down = cat([piece[5][:32], down + piece[5][32:]])
    up = send(up.astype(BF), "z", 1).astype(F32)
    down = send(down.astype(BF), "z", -1).astype(F32)
    up = send((up + piece[2]).astype(BF), "z", 1).astype(F32)
    down = send((down + piece[6]).astype(BF), "z", -1).astype(F32)
    grad_out, grad_in_t = call(
        own_kernel, [shape((h, d), F32)] * 2, [me, after(full, pair), tok, cot], flops
    )
    up = send((up + piece[1]).astype(BF), "z", 1).astype(F32)
    down = send((down + piece[7]).astype(BF), "z", -1).astype(F32)
    total = piece[0] + up + down
    far = send(cat([total[16:32], total[48:]]).astype(BF), "x", 2).astype(F32)
    output = (total[:16] + far[:16]).astype(BF)
    input_grad = (total[32:48] + far[16:]).astype(BF)
    grad_out = grad_out + pair[:h].astype(F32)
    grad_in_t = grad_in_t + pair[h:].astype(F32)
    return (output, input_grad, grad_in_t.T, grad_out)


def solution(mesh):
    mesh = Mesh(mesh.devices.reshape(8, 4, 4, 2), ("z", "x", "row", "col"))
    whole = ("z", "x", "col")
    placed = (P(whole, "row"), P("row", whole), P(whole, "row"), P(whole, "row"))
    return jax.shard_map(
        on_device,
        mesh=mesh,
        in_specs=placed,
        out_specs=(P(whole, "row"), P(whole, "row"), P("row", whole), P(whole, "row")),
        check_vma=False,
    )
```

```python
import functools

import jax
import jax.numpy as jnp
from jax import lax
from jax.experimental import pallas as pl
from jax.experimental.pallas import tpu as pltpu
from jax.sharding import Mesh, PartitionSpec as P

BF = jnp.bfloat16
F32 = jnp.float32
SIZE = {"z": 8, "x": 4, "row": 4, "col": 2}
ORDER = (0, 1, 7, 2, 6, 3, 5, 4)
HEAD = 5


def smooth_gate(value):
    return 0.5 * value * (1.0 + lax.erf(value * 0.7071067811865476))


def smooth_slope(value):
    cumul = 0.5 * (1.0 + lax.erf(value * 0.7071067811865476))
    return cumul + value * jnp.exp(-0.5 * value * value) * 0.3989422804014327


def send(value, axis, shift):
    size = SIZE[axis]
    return lax.ppermute(value, axis, [(i, (i + shift) % size) for i in range(size)])


def token_pair(value):
    return lax.ppermute(value, "x", [(0, 1), (1, 0), (2, 3), (3, 2)])


def weight_pair(value):
    return lax.ppermute(value, "x", [(0, 3), (3, 0), (1, 2), (2, 1)])


def after(value, other):
    return lax.optimization_barrier((value, other))[0]


def call(body, outs, args, flops=1 << 20, scratch=()):
    specs = [pl.BlockSpec(memory_space=pltpu.SMEM)]
    specs += [pl.BlockSpec(memory_space=pltpu.VMEM)] * (len(args) - 1)
    kernel = pl.pallas_call(
        body,
        out_shape=outs,
        in_specs=specs,
        out_specs=[pl.BlockSpec(memory_space=pltpu.VMEM)] * len(outs),
        scratch_shapes=list(scratch),
        compiler_params=pltpu.CompilerParams(vmem_limit_bytes=40 << 20),
        cost_estimate=pl.CostEstimate(
            flops=flops, bytes_accessed=1 << 20, transcendentals=0
        ),
    )
    return list(kernel(*args))


def cat(values):
    return jnp.concatenate(values, 0)


def dot(a, b, dim_a, dim_b):
    return lax.dot_general(
        a, b, (((dim_a,), (dim_b,)), ((), ())), preferred_element_type=F32
    )


def up_kernel(me, *refs):
    quarters, weights = refs[:8], (refs[8:10], refs[10:12])
    tok, cot, parts, whole = refs[12], refs[13], refs[14:18], refs[18]
    h = weights[0][0].shape[0]
    for q in range(4):
        for j in range(8):
            ref, i = (quarters[2 * q], j) if j < HEAD else (quarters[2 * q + 1], j - HEAD)
            row = q * 128 + j * 16
            tok[row : row + 16] = ref[i * 32 : i * 32 + 16]
            cot[row : row + 16] = ref[i * 32 + 16 : i * 32 + 32]
    for s, value in enumerate((tok, cot)):
        for i, w in enumerate(weights[s]):
            total = dot(w[...], value[...], 1, 1)
            for q in range(4):
                whole[q, s, i * h : i * h + h] = total[:, q * 128 : q * 128 + 128]
    for k, part in enumerate(parts):
        part[...] = whole[(me[0] + k) % 4]


def act_kernel(me, p0, p1, p2, p3, out):
    del me
    pre = p0[0] + p1[0] + p2[0] + p3[0]
    grad_act = p0[1] + p1[1] + p2[1] + p3[1]
    out[0] = smooth_gate(pre).astype(BF)
    out[1] = (grad_act * smooth_slope(pre)).astype(BF)


def down_kernel(me, b0, b1, b2, b3, wi, wi2, wo, wo2, near, far, head, tail, full):
    h = wi.shape[0]
    for k, block in enumerate((b0, b1, b2, b3)):
        lane = pl.multiple_of(((me[0] + k) % 4) * 128, 128)
        full[:, :, pl.ds(lane, 128)] = block[...]
    for s, (w, w2) in enumerate(((wo, wo2), (wi, wi2))):
        value = dot(full[s, :h], w[...], 0, 0) + dot(full[s, h:], w2[...], 0, 0)
        for q in range(4):
            for j in range(8):
                piece = value[q * 128 + j * 16 : q * 128 + j * 16 + 16]
                row = j * 32 + s * 16
                if q < 2:
                    (near, far)[q][row : row + 16] = piece
                elif j < HEAD:
                    row += (3 - q) * HEAD * 32
                    head[row : row + 16] = piece.astype(BF)
                else:
                    row += (3 - q) * (8 - HEAD) * 32 - HEAD * 32
                    tail[row : row + 16] = piece.astype(BF)


def pair_kernel(me, full, tok, cot, out, back):
    del me
    h = full.shape[1] // 2
    out[...] = dot(full[0, h:], cot[...], 1, 0).astype(BF)
    back[...] = dot(full[1, h:], tok[...], 1, 0).astype(BF)


def own_kernel(s, me, full, value, other, grad):
    del me
    h = full.shape[1] // 2
    grad[...] = dot(full[s, :h], value[...], 1, 0) + other[...].astype(F32)


def on_device(tokens, w_in, w_out, cotangent):
    me = lax.axis_index("row").astype(jnp.int32).reshape(1)
    d, h = w_in.shape
    shape = jax.ShapeDtypeStruct
    flops = 2 * 1024 * d * h

    z = {0: cat([tokens, cotangent])}
    z[1], z[7] = send(z[0], "z", -1), send(z[0], "z", 1)
    w_in_t = w_in.T
    w_in_2 = weight_pair(after(w_in_t, z[0]))
    z[2], z[6] = send(z[1], "z", -1), send(z[7], "z", 1)
    near_h = cat([z[k] for k in ORDER[:HEAD]])
    ring = after((z[2], z[6]), w_in_2)
    w_out_2 = weight_pair(after(w_out, z[2]))
    far_h = token_pair(near_h)
    z[3], z[5] = send(ring[0], "z", -1), send(ring[1], "z", 1)
    ring = after((z[3], z[5]), w_out_2)
    z[4] = cat([send(ring[0][:16], "z", -1), send(ring[1][16:], "z", 1)])
    near_t = cat([z[k] for k in ORDER[HEAD:]])
    far_t = token_pair(near_t)
    quarters = [near_h, near_t, far_h, far_t]
    quarters += [send(value, "col", 1) for value in quarters]

    part = shape((2, 2 * h, 128), F32)
    tok, cot, *parts = call(
        up_kernel,
        [shape((512, d), BF)] * 2 + [part] * 4,
        [me, *quarters, w_in_t, w_in_2, w_out, w_out_2],
        2 * flops,
        [pltpu.VMEM((4, 2, 2 * h, 128), F32)],
    )
    parts[1:] = [send(parts[k], "row", k) for k in (1, 2, 3)]
    (block,) = call(act_kernel, [shape((2, 2 * h, 128), BF)], [me, *parts])
    blocks = [block] + [send(block, "row", -k) for k in (1, 2, 3)]

    sums = shape((256, d), F32)
    near, far, head, tail, full = call(
        down_kernel,
        [sums, sums, shape((HEAD * 64, d), BF), shape(((8 - HEAD) * 64, d), BF), shape((2, 2 * h, 512), BF)],
        [me, *blocks, w_in_t, w_in_2, w_out, w_out_2],
        2 * flops,
    )
    cut, rest = HEAD * 32, (8 - HEAD) * 32
    tail = send(tail, "col", 1).astype(F32)
    far_t = token_pair((far[cut:] + tail[:rest]).astype(BF)).astype(F32)
    near_t = near[cut:] + tail[rest:] + far_t
    head = send(head, "col", 1).astype(F32)
    far_h = token_pair((far[:cut] + head[:cut]).astype(BF)).astype(F32)
    near_h = near[:cut] + head[cut:] + far_h
    piece = {}
    for i, k in enumerate(ORDER):
        piece[k] = near_h[i * 32 : i * 32 + 32] if i < HEAD else near_t[(i - HEAD) * 32 : (i - HEAD) * 32 + 32]
    pair_out, pair_in = call(
        pair_kernel, [shape((h, d), BF)] * 2, [me, after(full, tail), tok, cot], flops
    )
    pair_out, pair_in = weight_pair(pair_out), weight_pair(pair_in)
    up = send(piece[4][:16].astype(BF), "z", 1).astype(F32)
    down = send(piece[4][16:].astype(BF), "z", -1).astype(F32)
    up = cat([up + piece[3][:16], piece[3][16:]]).astype(BF)
    down = cat([piece[5][:16], down + piece[5][16:]]).astype(BF)
    up, down = after((up, down), pair_out)
    up, down = send(up, "z", 1).astype(F32), send(down, "z", -1).astype(F32)
    up, down = (up + piece[2]).astype(BF), (down + piece[6]).astype(BF)
    up, down = after((up, down), pair_in)
    up, down = send(up, "z", 1).astype(F32), send(down, "z", -1).astype(F32)
    weight = [shape((h, d), F32)]
    (grad_out,) = call(functools.partial(own_kernel, 0), weight, [me, full, cot, pair_out], flops)
    (grad_in_t,) = call(functools.partial(own_kernel, 1), weight, [me, full, tok, pair_in], flops)
    up, down = (up + piece[1]).astype(BF), (down + piece[7]).astype(BF)
    up, down = send(up, "z", 1).astype(F32), send(down, "z", -1).astype(F32)
    total = (piece[0] + up + down).astype(BF)
    output, input_grad = total[:16], total[16:]
    return (output, input_grad, grad_in_t.T, grad_out)


def solution(mesh):
    mesh = Mesh(mesh.devices.reshape(8, 4, 4, 2), ("z", "x", "row", "col"))
    whole = ("z", "x", "col")
    placed = (P(whole, "row"), P("row", whole), P(whole, "row"), P(whole, "row"))
    return jax.shard_map(
        on_device,
        mesh=mesh,
        in_specs=placed,
        out_specs=(P(whole, "row"), P(whole, "row"), P("row", whole), P(whole, "row")),
        check_vma=False,
    )
```

```python
import functools

import jax
import jax.numpy as jnp
from jax import lax
from jax.experimental import pallas as pl
from jax.experimental.pallas import tpu as pltpu
from jax.sharding import Mesh, PartitionSpec as P

BF = jnp.bfloat16
F32 = jnp.float32
SIZE = {"z": 8, "x": 4, "row": 4, "col": 2}
ORDER = (0, 1, 7, 2, 6, 3, 5, 4)
HEAD = 5


def smooth_gate(value):
    return 0.5 * value * (1.0 + lax.erf(value * 0.7071067811865476))


def smooth_slope(value):
    cumul = 0.5 * (1.0 + lax.erf(value * 0.7071067811865476))
    return cumul + value * jnp.exp(-0.5 * value * value) * 0.3989422804014327


def send(value, axis, shift):
    size = SIZE[axis]
    return lax.ppermute(value, axis, [(i, (i + shift) % size) for i in range(size)])


def token_pair(value):
    return lax.ppermute(value, "x", [(0, 1), (1, 0), (2, 3), (3, 2)])


def weight_pair(value):
    return lax.ppermute(value, "x", [(0, 3), (3, 0), (1, 2), (2, 1)])


def after(value, other):
    return lax.optimization_barrier((value, other))[0]


def call(body, outs, args, flops=1 << 20, scratch=()):
    specs = [pl.BlockSpec(memory_space=pltpu.SMEM)]
    specs += [pl.BlockSpec(memory_space=pltpu.VMEM)] * (len(args) - 1)
    kernel = pl.pallas_call(
        body,
        out_shape=outs,
        in_specs=specs,
        out_specs=[pl.BlockSpec(memory_space=pltpu.VMEM)] * len(outs),
        scratch_shapes=list(scratch),
        compiler_params=pltpu.CompilerParams(vmem_limit_bytes=40 << 20),
        cost_estimate=pl.CostEstimate(
            flops=flops, bytes_accessed=1 << 20, transcendentals=0
        ),
    )
    return list(kernel(*args))


def cat(values):
    return jnp.concatenate(values, 0)


def dot(a, b, dim_a, dim_b):
    return lax.dot_general(
        a, b, (((dim_a,), (dim_b,)), ((), ())), preferred_element_type=F32
    )


def up_kernel(me, *refs):
    quarters, weights = refs[:8], (refs[8:10], refs[10:12])
    tok, cot, parts, whole = refs[12], refs[13], refs[14:18], refs[18]
    h = weights[0][0].shape[0]
    for q in range(4):
        for j in range(8):
            ref, i = (quarters[2 * q], j) if j < HEAD else (quarters[2 * q + 1], j - HEAD)
            row = q * 128 + j * 16
            tok[row : row + 16] = ref[i * 32 : i * 32 + 16]
            cot[row : row + 16] = ref[i * 32 + 16 : i * 32 + 32]
    for s, value in enumerate((tok, cot)):
        for i, w in enumerate(weights[s]):
            total = dot(w[...], value[...], 1, 1)
            for q in range(4):
                whole[q, s, i * h : i * h + h] = total[:, q * 128 : q * 128 + 128]
    for k, part in enumerate(parts):
        part[...] = whole[(me[0] + k) % 4].astype(part.dtype)


def act_kernel(me, p0, p1, p2, p3, out):
    del me
    pre, grad_act = p0[0], p0[1]
    for part in (p1, p2, p3):
        pre += part[0].astype(F32)
        grad_act += part[1].astype(F32)
    out[0] = smooth_gate(pre).astype(BF)
    out[1] = (grad_act * smooth_slope(pre)).astype(BF)


def down_kernel(me, b0, b1, b2, b3, wi, wi2, wo, wo2, near, far, head, tail, full):
    h = wi.shape[0]
    for k, block in enumerate((b0, b1, b2, b3)):
        lane = pl.multiple_of(((me[0] + k) % 4) * 128, 128)
        full[:, :, pl.ds(lane, 128)] = block[...]
    for s, (w, w2) in enumerate(((wo, wo2), (wi, wi2))):
        value = dot(full[s, :h], w[...], 0, 0) + dot(full[s, h:], w2[...], 0, 0)
        for q in range(4):
            for j in range(8):
                piece = value[q * 128 + j * 16 : q * 128 + j * 16 + 16]
                row = j * 32 + s * 16
                if q < 2:
                    (near, far)[q][row : row + 16] = piece
                elif j < HEAD:
                    row += (3 - q) * HEAD * 32
                    head[row : row + 16] = piece.astype(BF)
                else:
                    row += (3 - q) * (8 - HEAD) * 32 - HEAD * 32
                    tail[row : row + 16] = piece.astype(BF)


def pair_kernel(me, full, tok, cot, out, back):
    del me
    h = full.shape[1] // 2
    out[...] = dot(full[0, h:], cot[...], 1, 0).astype(BF)
    back[...] = dot(full[1, h:], tok[...], 1, 0).astype(BF)


def own_kernel(s, me, full, value, other, grad):
    del me
    h = full.shape[1] // 2
    grad[...] = dot(full[s, :h], value[...], 1, 0) + other[...].astype(F32)


def on_device(tokens, w_in, w_out, cotangent):
    me = lax.axis_index("row").astype(jnp.int32).reshape(1)
    d, h = w_in.shape
    shape = jax.ShapeDtypeStruct
    flops = 2 * 1024 * d * h

    z = {0: cat([tokens, cotangent])}
    z[1], z[7] = send(z[0], "z", -1), send(z[0], "z", 1)
    w_in_t = w_in.T
    w_in_2 = weight_pair(after(w_in_t, z[0]))
    z[2], z[6] = send(z[1], "z", -1), send(z[7], "z", 1)
    near_h = cat([z[k] for k in ORDER[:HEAD]])
    ring = after((z[2], z[6]), w_in_2)
    w_out_2 = weight_pair(after(w_out, z[2]))
    far_h = token_pair(near_h)
    z[3], z[5] = send(ring[0], "z", -1), send(ring[1], "z", 1)
    ring = after((z[3], z[5]), w_out_2)
    z[4] = cat([send(ring[0][:16], "z", -1), send(ring[1][16:], "z", 1)])
    near_t = cat([z[k] for k in ORDER[HEAD:]])
    far_t = token_pair(near_t)
    quarters = [near_h, near_t, far_h, far_t]
    quarters += [send(value, "col", 1) for value in quarters]

    part, rounded = shape((2, 2 * h, 128), F32), shape((2, 2 * h, 128), BF)
    tok, cot, *parts = call(
        up_kernel,
        [shape((512, d), BF)] * 2 + [part] + [rounded] * 3,
        [me, *quarters, w_in_t, w_in_2, w_out, w_out_2],
        2 * flops,
        [pltpu.VMEM((4, 2, 2 * h, 128), F32)],
    )
    parts[1:] = [send(parts[k], "row", k) for k in (1, 2, 3)]
    (block,) = call(act_kernel, [rounded], [me, *parts])
    blocks = [block] + [send(block, "row", -k) for k in (1, 2, 3)]

    sums = shape((256, d), F32)
    near, far, head, tail, full = call(
        down_kernel,
        [sums, sums, shape((HEAD * 64, d), BF), shape(((8 - HEAD) * 64, d), BF), shape((2, 2 * h, 512), BF)],
        [me, *blocks, w_in_t, w_in_2, w_out, w_out_2],
        2 * flops,
    )
    cut, rest = HEAD * 32, (8 - HEAD) * 32
    tail = send(tail, "col", 1).astype(F32)
    far_t = token_pair((far[cut:] + tail[:rest]).astype(BF)).astype(F32)
    near_t = near[cut:] + tail[rest:] + far_t
    head = send(head, "col", 1).astype(F32)
    far_h = (far[:cut] + head[:cut]).astype(BF)
    first = after(near_t[-32:], far_h)
    far_h = token_pair(far_h).astype(F32)
    near_h = near[:cut] + head[cut:] + far_h
    piece = {}
    for i, k in enumerate(ORDER):
        piece[k] = near_h[i * 32 : i * 32 + 32] if i < HEAD else near_t[(i - HEAD) * 32 : (i - HEAD) * 32 + 32]
    pair_out, pair_in = call(
        pair_kernel, [shape((h, d), BF)] * 2, [me, after(full, tail), tok, cot], flops
    )
    pair_out, pair_in = weight_pair(pair_out), weight_pair(pair_in)
    up = send(first[:16].astype(BF), "z", 1).astype(F32)
    down = send(first[16:].astype(BF), "z", -1).astype(F32)
    up = cat([up + piece[3][:16], piece[3][16:]]).astype(BF)
    down = cat([piece[5][:16], down + piece[5][16:]]).astype(BF)
    up, down = after((up, down), pair_out)
    up, down = send(up, "z", 1).astype(F32), send(down, "z", -1).astype(F32)
    up, down = (up + piece[2]).astype(BF), (down + piece[6]).astype(BF)
    up, down = after((up, down), pair_in)
    up, down = send(up, "z", 1).astype(F32), send(down, "z", -1).astype(F32)
    weight = [shape((h, d), F32)]
    (grad_out,) = call(functools.partial(own_kernel, 0), weight, [me, full, cot, pair_out], flops)
    (grad_in_t,) = call(functools.partial(own_kernel, 1), weight, [me, full, tok, pair_in], flops)
    up, down = after((up + piece[1], down + piece[7]), grad_out)
    up, down = send(up, "z", 1), send(down, "z", -1)
    total = (piece[0] + up + down).astype(BF)
    output, input_grad = total[:16], total[16:]
    return (output, input_grad, grad_in_t.T, grad_out)


def solution(mesh):
    mesh = Mesh(mesh.devices.reshape(8, 4, 4, 2), ("z", "x", "row", "col"))
    whole = ("z", "x", "col")
    placed = (P(whole, "row"), P("row", whole), P(whole, "row"), P(whole, "row"))
    return jax.shard_map(
        on_device,
        mesh=mesh,
        in_specs=placed,
        out_specs=(P(whole, "row"), P(whole, "row"), P("row", whole), P(whole, "row")),
        check_vma=False,
    )
```

```python
import functools

import jax
import jax.numpy as jnp
from jax import lax
from jax.experimental import pallas as pl
from jax.experimental.pallas import tpu as pltpu
from jax.sharding import Mesh, PartitionSpec as P

BF = jnp.bfloat16
F32 = jnp.float32
SIZE = {"z": 8, "x": 4, "row": 4, "col": 2}
CUT, REST = 160, 96


def smooth_gate(value):
    return 0.5 * value * (1.0 + lax.erf(value * 0.7071067811865476))


def smooth_slope(value):
    cumul = 0.5 * (1.0 + lax.erf(value * 0.7071067811865476))
    return cumul + value * jnp.exp(-0.5 * value * value) * 0.3989422804014327


def send(value, axis, shift):
    size = SIZE[axis]
    return lax.ppermute(value, axis, [(i, (i + shift) % size) for i in range(size)])


def along(value):
    pairs = [(2 * i + c, (i + 1 - 2 * c) % 8 * 2 + c) for i in range(8) for c in range(2)]
    return lax.ppermute(value, ("z", "col"), pairs)


def token_pair(value):
    return lax.ppermute(value, "x", [(0, 1), (1, 0), (2, 3), (3, 2)])


def weight_pair(value):
    return lax.ppermute(value, "x", [(0, 3), (3, 0), (1, 2), (2, 1)])


def after(value, other):
    return lax.optimization_barrier((value, other))[0]


def call(body, outs, args, flops=1 << 20, scratch=()):
    specs = [pl.BlockSpec(memory_space=pltpu.SMEM)]
    specs += [pl.BlockSpec(memory_space=pltpu.VMEM)] * (len(args) - 1)
    kernel = pl.pallas_call(
        body,
        out_shape=outs,
        in_specs=specs,
        out_specs=[pl.BlockSpec(memory_space=pltpu.VMEM)] * len(outs),
        scratch_shapes=list(scratch),
        compiler_params=pltpu.CompilerParams(vmem_limit_bytes=40 << 20),
        cost_estimate=pl.CostEstimate(
            flops=flops, bytes_accessed=1 << 20, transcendentals=0
        ),
    )
    return list(kernel(*args))


def cat(values):
    return jnp.concatenate(values, 0)


def dot(a, b, dim_a, dim_b):
    return lax.dot_general(
        a, b, (((dim_a,), (dim_b,)), ((), ())), preferred_element_type=F32
    )


def blocks(core, sign):
    out = [(0, core, 0)]
    for step in (1, 2, 3):
        z = (8 + sign * (1 - 2 * core) * step) % 8
        out += [(64 * step - 32, core, z), (64 * step, 1 - core, z)]
    return out + [(224, core, 4)]


def place(chip, core, z):
    return pl.ds(pl.multiple_of(chip * 256 + core * 128 + z * 16, 16), 16)


def up_kernel(me, *refs):
    held, weights = refs[:8], (refs[8:10], refs[10:12])
    tok, cot, parts, whole = refs[12], refs[13], refs[14:18], refs[18]
    h = weights[0][0].shape[0]
    for group in range(2):
        mine = me[1] if group == 0 else 1 - me[1]
        for chip in range(2):
            pair = held[group * 4 + chip * 2 : group * 4 + chip * 2 + 2]
            for row, core, z in blocks(mine, -1):
                ref, row = (pair[0], row) if row < CUT else (pair[1], row - CUT)
                tok[place(chip, core, z)] = ref[row : row + 16]
                cot[place(chip, core, z)] = ref[row + 16 : row + 32]
    for s, value in enumerate((tok, cot)):
        for i, w in enumerate(weights[s]):
            total = dot(w[...], value[...], 1, 1)
            for q in range(4):
                whole[q, s, i * h : i * h + h] = total[:, q * 128 : q * 128 + 128]
    for k, part in enumerate(parts):
        part[...] = whole[(me[0] + k) % 4].astype(part.dtype)


def act_kernel(me, p0, p1, p2, p3, out):
    del me
    pre, grad_act = p0[0], p0[1]
    for part in (p1, p2, p3):
        pre += part[0].astype(F32)
        grad_act += part[1].astype(F32)
    out[0] = smooth_gate(pre).astype(BF)
    out[1] = (grad_act * smooth_slope(pre)).astype(BF)


def down_kernel(me, b0, b1, b2, b3, wi, wi2, wo, wo2, near, far, head, tail, full, whole):
    h = wi.shape[0]
    for k, block in enumerate((b0, b1, b2, b3)):
        lane = pl.multiple_of(((me[0] + k) % 4) * 128, 128)
        full[:, :, pl.ds(lane, 128)] = block[...]
    for s, (w, w2) in enumerate(((wo, wo2), (wi, wi2))):
        whole[...] = dot(full[s, :h], w[...], 0, 0) + dot(full[s, h:], w2[...], 0, 0)
        for chip in range(2):
            for row, core, z in blocks(1 - me[1], 1):
                value = whole[place(chip, core, z)].astype(BF)
                if row < CUT:
                    row += (1 - chip) * CUT + s * 16
                    head[row : row + 16] = value
                else:
                    row += (1 - chip) * REST - CUT + s * 16
                    tail[row : row + 16] = value
            for row, core, z in blocks(me[1], 1):
                (near, far)[chip][row + s * 16 : row + s * 16 + 16] = whole[place(chip, core, z)]


def pair_kernel(me, full, tok, cot, out, back):
    del me
    h = full.shape[1] // 2
    out[...] = dot(full[0, h:], cot[...], 1, 0).astype(BF)
    back[...] = dot(full[1, h:], tok[...], 1, 0).astype(BF)


def own_kernel(s, me, full, value, other, grad):
    del me
    h = full.shape[1] // 2
    grad[...] = dot(full[s, :h], value[...], 1, 0) + other[...].astype(F32)


def on_device(tokens, w_in, w_out, cotangent):
    me = jnp.stack([lax.axis_index("row"), lax.axis_index("col")]).astype(jnp.int32)
    d, h = w_in.shape
    shape = jax.ShapeDtypeStruct
    flops = 2 * 1024 * d * h

    base = cat([tokens, cotangent])
    first = along(cat([base, send(base, "col", 1)]))
    w_in_t = w_in.T
    w_in_2 = weight_pair(after(w_in_t, base))
    second = along(first)
    near_h = cat([base, first, second])
    third = after(second, w_in_2)
    w_out_2 = weight_pair(after(w_out, second))
    far_h = token_pair(near_h)
    third = along(third)
    near_t = cat([third, along(after(third, w_out_2)[:32])])
    far_t = token_pair(near_t)
    quarters = [near_h, near_t, far_h, far_t]
    quarters += [send(value, "col", 1) for value in quarters]

    part, rounded = shape((2, 2 * h, 128), F32), shape((2, 2 * h, 128), BF)
    tok, cot, *parts = call(
        up_kernel,
        [shape((512, d), BF)] * 2 + [part] + [rounded] * 3,
        [me, *quarters, w_in_t, w_in_2, w_out, w_out_2],
        2 * flops,
        [pltpu.VMEM((4, 2, 2 * h, 128), F32)],
    )
    parts[1:] = [send(parts[k], "row", k) for k in (1, 2, 3)]
    (block,) = call(act_kernel, [rounded], [me, *parts])
    shared = [block] + [send(block, "row", -k) for k in (1, 2, 3)]

    sums = shape((256, d), F32)
    near, far, head, tail, full = call(
        down_kernel,
        [sums, sums, shape((2 * CUT, d), BF), shape((2 * REST, d), BF), shape((2, 2 * h, 512), BF)],
        [me, *shared, w_in_t, w_in_2, w_out, w_out_2],
        2 * flops,
        [pltpu.VMEM((512, d), F32)],
    )
    tail = send(tail, "col", 1).astype(F32)
    far_t = token_pair((far[CUT:] + tail[:REST]).astype(BF)).astype(F32)
    near_t = near[CUT:] + tail[REST:] + far_t
    head = send(head, "col", 1).astype(F32)
    far_h = (far[:CUT] + head[:CUT]).astype(BF)
    chain = after(near_t[64:], far_h)
    near_h = near[:CUT] + head[CUT:] + token_pair(far_h).astype(F32)
    pair_out, pair_in = call(
        pair_kernel, [shape((h, d), BF)] * 2, [me, after(full, tail), tok, cot], flops
    )
    pair_out, pair_in = weight_pair(pair_out), weight_pair(pair_in)
    chain = along(chain.astype(BF)).astype(F32)
    chain = cat([near_t[:32] + chain, near_t[32:64]]).astype(BF)
    chain = along(after(chain, pair_out)).astype(F32)
    chain = (near_h[96:160] + chain).astype(BF)
    chain = along(after(chain, pair_in)).astype(F32)
    weight = [shape((h, d), F32)]
    (grad_out,) = call(functools.partial(own_kernel, 0), weight, [me, full, cot, pair_out], flops)
    (grad_in_t,) = call(functools.partial(own_kernel, 1), weight, [me, full, tok, pair_in], flops)
    chain = along(after(near_h[32:96] + chain, grad_out))
    total = near_h[:32] + chain[:32] + send(after(chain[32:], grad_in_t), "col", 1)
    output, input_grad = total[:16].astype(BF), total[16:].astype(BF)
    return (output, input_grad, grad_in_t.T, grad_out)


def solution(mesh):
    mesh = Mesh(mesh.devices.reshape(8, 4, 4, 2), ("z", "x", "row", "col"))
    whole = ("z", "x", "col")
    placed = (P(whole, "row"), P("row", whole), P(whole, "row"), P(whole, "row"))
    return jax.shard_map(
        on_device,
        mesh=mesh,
        in_specs=placed,
        out_specs=(P(whole, "row"), P(whole, "row"), P("row", whole), P(whole, "row")),
        check_vma=False,
    )
```

```python
import jax
import jax.numpy as jnp
from jax import lax
from jax.experimental import pallas as pl
from jax.experimental.pallas import tpu as pltpu
from jax.sharding import Mesh, PartitionSpec as P

BF = jnp.bfloat16
F32 = jnp.float32
SIZE = {"z": 8, "x": 4, "row": 4, "col": 2}
ORDER = (0, 1, 7, 2, 6, 3, 5, 4)
HEAD = 5


def smooth_gate(value):
    return 0.5 * value * (1.0 + lax.erf(value * 0.7071067811865476))


def smooth_slope(value):
    cumul = 0.5 * (1.0 + lax.erf(value * 0.7071067811865476))
    return cumul + value * jnp.exp(-0.5 * value * value) * 0.3989422804014327


def send(value, axis, shift):
    size = SIZE[axis]
    return lax.ppermute(value, axis, [(i, (i + shift) % size) for i in range(size)])


def token_pair(value):
    return lax.ppermute(value, "x", [(0, 1), (1, 0), (2, 3), (3, 2)])


def weight_pair(value):
    return lax.ppermute(value, "x", [(0, 3), (3, 0), (1, 2), (2, 1)])


def after(value, other):
    return lax.optimization_barrier((value, other))[0]


def call(body, outs, args, flops=1 << 20, scratch=()):
    specs = [pl.BlockSpec(memory_space=pltpu.SMEM)]
    specs += [pl.BlockSpec(memory_space=pltpu.VMEM)] * (len(args) - 1)
    kernel = pl.pallas_call(
        body,
        out_shape=outs,
        in_specs=specs,
        out_specs=[pl.BlockSpec(memory_space=pltpu.VMEM)] * len(outs),
        scratch_shapes=list(scratch),
        compiler_params=pltpu.CompilerParams(vmem_limit_bytes=40 << 20),
        cost_estimate=pl.CostEstimate(
            flops=flops, bytes_accessed=1 << 20, transcendentals=0
        ),
    )
    return list(kernel(*args))


def cat(values):
    return jnp.concatenate(values, 0)


def dot(a, b, dim_a, dim_b):
    return lax.dot_general(
        a, b, (((dim_a,), (dim_b,)), ((), ())), preferred_element_type=F32
    )


def up_kernel(me, *refs):
    quarters, weights = refs[:8], (refs[8:10], refs[10:12])
    tok, cot, parts, whole = refs[12], refs[13], refs[14:18], refs[18]
    h = weights[0][0].shape[0]
    for q in range(4):
        for j in range(8):
            ref, i = (quarters[2 * q], j) if j < HEAD else (quarters[2 * q + 1], j - HEAD)
            row = q * 128 + j * 16
            tok[row : row + 16] = ref[i * 32 : i * 32 + 16]
            cot[row : row + 16] = ref[i * 32 + 16 : i * 32 + 32]
    for s, value in enumerate((tok, cot)):
        for i, w in enumerate(weights[s]):
            total = dot(w[...], value[...], 1, 1)
            for q in range(4):
                whole[q, s, i * h : i * h + h] = total[:, q * 128 : q * 128 + 128]
    for k, part in enumerate(parts):
        part[...] = whole[(me[0] + k) % 4].astype(part.dtype)


def act_kernel(me, p0, p1, p2, p3, out):
    del me
    pre, grad_act = p0[0], p0[1]
    for part in (p1, p2, p3):
        pre += part[0].astype(F32)
        grad_act += part[1].astype(F32)
    out[0] = smooth_gate(pre).astype(BF)
    out[1] = (grad_act * smooth_slope(pre)).astype(BF)


def down_kernel(me, full, wi, wi2, wo, wo2, near, far, head, tail):
    del me
    h = wi.shape[0]
    for s, (w, w2) in enumerate(((wo, wo2), (wi, wi2))):
        value = dot(full[s, :h], w[...], 0, 0) + dot(full[s, h:], w2[...], 0, 0)
        for q in range(4):
            for j in range(8):
                piece = value[q * 128 + j * 16 : q * 128 + j * 16 + 16]
                row = j * 32 + s * 16
                if q < 2:
                    (near, far)[q][row : row + 16] = piece
                elif j < HEAD:
                    row += (3 - q) * HEAD * 32
                    head[row : row + 16] = piece.astype(BF)
                else:
                    row += (3 - q) * (8 - HEAD) * 32 - HEAD * 32
                    tail[row : row + 16] = piece.astype(BF)


def pair_kernel(me, b0, b1, b2, b3, tok, cot, full, out, back):
    h = full.shape[1] // 2
    for k, block in enumerate((b0, b1, b2, b3)):
        lane = pl.multiple_of(((me[0] + k) % 4) * 128, 128)
        full[:, :, pl.ds(lane, 128)] = block[...]
    out[...] = dot(full[0, h:], cot[...], 1, 0).astype(BF)
    back[...] = dot(full[1, h:], tok[...], 1, 0).astype(BF)


def own_kernel(me, full, tok, cot, grad_out, grad_in):
    del me
    h = full.shape[1] // 2
    grad_out[...] = dot(full[0, :h], cot[...], 1, 0)
    grad_in[...] = dot(full[1, :h], tok[...], 1, 0)


def on_device(tokens, w_in, w_out, cotangent):
    me = lax.axis_index("row").astype(jnp.int32).reshape(1)
    d, h = w_in.shape
    shape = jax.ShapeDtypeStruct
    flops = 2 * 1024 * d * h

    base = cat([tokens, cotangent])
    z = {0: base}
    z[2], z[6] = send(base, "z", -2), send(base, "z", 2)
    z[1], z[7] = send(base, "z", -1), send(base, "z", 1)
    w_in_t = w_in.T
    w_in_2 = weight_pair(after(w_in_t, base))
    z[3], z[5] = send(z[2], "z", -1), send(z[6], "z", 1)
    z[4] = cat([send(z[2][:16], "z", -2), send(z[6][16:], "z", 2)])
    w_out_2 = weight_pair(after(w_out, (z[2], z[6])))
    near_h = cat([z[k] for k in ORDER[:HEAD]])
    far_h = token_pair(near_h)
    near_t = cat([z[k] for k in ORDER[HEAD:]])
    far_t = token_pair(after(near_t, w_in_2))
    far_h = after(far_h, w_out_2)
    quarters = [near_h, near_t, far_h, far_t]
    quarters += [send(value, "col", 1) for value in quarters]

    part, rounded = shape((2, 2 * h, 128), F32), shape((2, 2 * h, 128), BF)
    tok, cot, *parts = call(
        up_kernel,
        [shape((512, d), BF)] * 2 + [part] + [rounded] * 3,
        [me, *quarters, w_in_t, w_in_2, w_out, w_out_2],
        2 * flops,
        [pltpu.VMEM((4, 2, 2 * h, 128), F32)],
    )
    parts[1:] = [send(parts[k], "row", k) for k in (1, 2, 3)]
    (block,) = call(act_kernel, [rounded], [me, *parts])
    blocks = [block] + [send(block, "row", -k) for k in (1, 2, 3)]

    sums = shape((256, d), F32)
    full, pair_out, pair_in = call(
        pair_kernel,
        [shape((2, 2 * h, 512), BF)] + [shape((h, d), BF)] * 2,
        [me, *blocks, tok, cot],
        flops,
    )
    near, far, head, tail = call(
        down_kernel,
        [sums, sums, shape((HEAD * 64, d), BF), shape(((8 - HEAD) * 64, d), BF)],
        [me, full, w_in_t, w_in_2, w_out, w_out_2],
        2 * flops,
    )
    cut, rest = HEAD * 32, (8 - HEAD) * 32
    tail = send(tail, "col", 1).astype(F32)
    head = send(head, "col", 1).astype(F32)
    far_t = (far[cut:] + tail[:rest]).astype(BF)
    far_2 = (far[96:cut] + head[96:cut]).astype(BF)
    far_1 = (far[:96] + head[:96]).astype(BF)
    pair_out, pair_in = after((pair_out, pair_in), far_t)
    pair_out, pair_in = weight_pair(pair_out), weight_pair(pair_in)
    grad_out, grad_in_t = call(
        own_kernel, [shape((h, d), F32)] * 2, [me, full, after(tok, far_t), cot], flops
    )
    far_t, far_2 = token_pair(far_t), token_pair(after(far_2, grad_out))
    third = (near[cut:] + tail[rest:] + far_t.astype(F32)).astype(BF)
    near, head = after((near, head), third)
    far_1 = token_pair(after(far_1, third))
    near_2 = near[96:cut] + head[96 + cut :] + far_2.astype(F32)
    third = after(third, grad_out)
    up, down = send(third[:32], "z", 1), send(third[32:64], "z", -1)
    up_2, down_2 = send(third[64:80], "z", 2), send(third[80:], "z", -2)
    up, down = up.astype(F32), down.astype(F32)
    up = cat([up[:16] + up_2.astype(F32), up[16:]]) + near_2[:32]
    down = cat([down[:16], down[16:] + down_2.astype(F32)]) + near_2[32:]
    up, down = after((up.astype(BF), down.astype(BF)), pair_out)
    near, head = after((near, head), up)
    near_1 = near[:96] + head[cut : 96 + cut] + far_1.astype(F32)
    total = near_1[:32] + send(up, "z", 2).astype(F32) + send(down, "z", -2).astype(F32)
    up, down = after((near_1[32:64].astype(BF), near_1[64:].astype(BF)), (up, down))
    total += send(up, "z", 1).astype(F32) + send(down, "z", -1).astype(F32)
    output, input_grad = total[:16].astype(BF), total[16:].astype(BF)
    grad_out = grad_out + pair_out.astype(F32)
    grad_in_t = grad_in_t + pair_in.astype(F32)
    return (output, input_grad, grad_in_t.T, grad_out)


def solution(mesh):
    mesh = Mesh(mesh.devices.reshape(8, 4, 4, 2), ("z", "x", "row", "col"))
    whole = ("z", "x", "col")
    placed = (P(whole, "row"), P("row", whole), P(whole, "row"), P(whole, "row"))
    return jax.shard_map(
        on_device,
        mesh=mesh,
        in_specs=placed,
        out_specs=(P(whole, "row"), P(whole, "row"), P("row", whole), P(whole, "row")),
        check_vma=False,
    )
```

```python
import jax
import jax.numpy as jnp
from jax import lax
from jax.experimental import pallas as pl
from jax.experimental.pallas import tpu as pltpu
from jax.sharding import Mesh, PartitionSpec as P

BF = jnp.bfloat16
F32 = jnp.float32
SIZE = {"z": 8, "x": 4, "row": 4, "col": 2}
ORDER = (0, 1, 7, 2, 6, 3, 5, 4)
HEAD = 5


def smooth_gate(value):
    return 0.5 * value * (1.0 + lax.erf(value * 0.7071067811865476))


def smooth_slope(value):
    cumul = 0.5 * (1.0 + lax.erf(value * 0.7071067811865476))
    return cumul + value * jnp.exp(-0.5 * value * value) * 0.3989422804014327


def send(value, axis, shift):
    size = SIZE[axis]
    return lax.ppermute(value, axis, [(i, (i + shift) % size) for i in range(size)])


def token_pair(value):
    return lax.ppermute(value, "x", [(0, 1), (1, 0), (2, 3), (3, 2)])


def weight_pair(value):
    return lax.ppermute(value, "x", [(0, 3), (3, 0), (1, 2), (2, 1)])


def after(value, other):
    return lax.optimization_barrier((value, other))[0]


def call(body, outs, args, flops=1 << 20, scratch=()):
    specs = [pl.BlockSpec(memory_space=pltpu.SMEM)]
    specs += [pl.BlockSpec(memory_space=pltpu.VMEM)] * (len(args) - 1)
    kernel = pl.pallas_call(
        body,
        out_shape=outs,
        in_specs=specs,
        out_specs=[pl.BlockSpec(memory_space=pltpu.VMEM)] * len(outs),
        scratch_shapes=list(scratch),
        compiler_params=pltpu.CompilerParams(vmem_limit_bytes=40 << 20),
        cost_estimate=pl.CostEstimate(
            flops=flops, bytes_accessed=1 << 20, transcendentals=0
        ),
    )
    return list(kernel(*args))


def cat(values):
    return jnp.concatenate(values, 0)


def dot(a, b, dim_a, dim_b):
    return lax.dot_general(
        a, b, (((dim_a,), (dim_b,)), ((), ())), preferred_element_type=F32
    )


def up_kernel(me, *refs):
    quarters, wi, wo, w_pair = refs[:8], refs[8], refs[9], refs[10]
    tok, cot, parts, whole = refs[11], refs[12], refs[13:17], refs[17]
    h = wi.shape[0]
    for q in range(4):
        for j in range(8):
            ref, i = (quarters[2 * q], j) if j < HEAD else (quarters[2 * q + 1], j - HEAD)
            row = q * 128 + j * 16
            tok[row : row + 16] = ref[i * 32 : i * 32 + 16]
            cot[row : row + 16] = ref[i * 32 + 16 : i * 32 + 32]
    for s, (w, value) in enumerate(((wi, tok), (wo, cot))):
        for i, left in enumerate((w[...], w_pair[s * h : s * h + h])):
            total = dot(left, value[...], 1, 1)
            for q in range(4):
                whole[q, s, i * h : i * h + h] = total[:, q * 128 : q * 128 + 128]
    for k, part in enumerate(parts):
        part[...] = whole[(me[0] + k) % 4].astype(part.dtype)


def act_kernel(me, p0, p1, p2, p3, out):
    del me
    pre, grad_act = p0[0], p0[1]
    for part in (p1, p2, p3):
        pre += part[0].astype(F32)
        grad_act += part[1].astype(F32)
    out[0] = smooth_gate(pre).astype(BF)
    out[1] = (grad_act * smooth_slope(pre)).astype(BF)


def down_kernel(me, full, wi, wo, w_pair, near, far, head, tail):
    del me
    h = wi.shape[0]
    for s, w in enumerate((wo, wi)):
        value = dot(full[s, :h], w[...], 0, 0)
        value += dot(full[s, h:], w_pair[(1 - s) * h : (2 - s) * h], 0, 0)
        for q in range(4):
            for j in range(8):
                piece = value[q * 128 + j * 16 : q * 128 + j * 16 + 16]
                row = j * 32 + s * 16
                if q < 2:
                    (near, far)[q][row : row + 16] = piece
                elif j < HEAD:
                    row += (3 - q) * HEAD * 32
                    head[row : row + 16] = piece.astype(BF)
                else:
                    row += (3 - q) * (8 - HEAD) * 32 - HEAD * 32
                    tail[row : row + 16] = piece.astype(BF)


def pair_kernel(me, b0, b1, b2, b3, tok, cot, full, out):
    h = full.shape[1] // 2
    for k, block in enumerate((b0, b1, b2, b3)):
        lane = pl.multiple_of(((me[0] + k) % 4) * 128, 128)
        full[:, :, pl.ds(lane, 128)] = block[...]
    out[:h] = dot(full[0, h:], cot[...], 1, 0).astype(BF)
    out[h:] = dot(full[1, h:], tok[...], 1, 0).astype(BF)


def own_kernel(me, full, tok, cot, grad_out, grad_in):
    del me
    h = full.shape[1] // 2
    grad_out[...] = dot(full[0, :h], cot[...], 1, 0)
    grad_in[...] = dot(full[1, :h], tok[...], 1, 0)


def on_device(tokens, w_in, w_out, cotangent):
    me = lax.axis_index("row").astype(jnp.int32).reshape(1)
    d, h = w_in.shape
    shape = jax.ShapeDtypeStruct
    flops = 2 * 1024 * d * h

    base = cat([tokens, cotangent])
    z = {0: base}
    z[2], z[6] = send(base, "z", -2), send(base, "z", 2)
    z[1], z[7] = send(base, "z", -1), send(base, "z", 1)
    w_in_t = w_in.T
    w_pair = weight_pair(after(cat([w_in_t, w_out]), base))
    z[3], z[5] = send(z[2], "z", -1), send(z[6], "z", 1)
    near_h = cat([z[k] for k in ORDER[:HEAD]])
    far_h = token_pair(near_h)
    z[4] = send(after(z[6], near_h), "z", 2)
    near_t = cat([z[k] for k in ORDER[HEAD:]])
    far_t = token_pair(near_t)
    far_h = after(far_h, w_pair)
    quarters = [near_h, near_t, far_h, far_t]
    quarters += [send(value, "col", 1) for value in quarters]

    part, rounded = shape((2, 2 * h, 128), F32), shape((2, 2 * h, 128), BF)
    tok, cot, *parts = call(
        up_kernel,
        [shape((512, d), BF)] * 2 + [part] + [rounded] * 3,
        [me, *quarters, w_in_t, w_out, w_pair],
        2 * flops,
        [pltpu.VMEM((4, 2, 2 * h, 128), F32)],
    )
    parts[1:] = [send(parts[k], "row", k) for k in (1, 2, 3)]
    (block,) = call(act_kernel, [rounded], [me, *parts])
    blocks = [block] + [send(block, "row", -k) for k in (1, 2, 3)]

    sums = shape((256, d), F32)
    full, pair = call(
        pair_kernel,
        [shape((2, 2 * h, 512), BF), shape((2 * h, d), BF)],
        [me, *blocks, tok, cot],
        flops,
    )
    near, far, head, tail = call(
        down_kernel,
        [sums, sums, shape((HEAD * 64, d), BF), shape(((8 - HEAD) * 64, d), BF)],
        [me, full, w_in_t, w_out, w_pair],
        2 * flops,
    )
    cut, rest = HEAD * 32, (8 - HEAD) * 32
    tail = send(tail, "col", 1)
    head = send(after(head, tail), "col", 1).astype(F32)
    tail = tail.astype(F32)
    far_t = (far[cut:] + tail[:rest]).astype(BF)
    far = after(far, far_t)
    pair = weight_pair(after(pair, far_t))
    grad_out, grad_in_t = call(
        own_kernel, [shape((h, d), F32)] * 2, [me, full, after(tok, far_t), cot], flops
    )
    far_t = token_pair(far_t)
    far_h = token_pair(after((far[:cut] + head[:cut]).astype(BF), grad_out))
    third = (near[cut:] + tail[rest:] + far_t.astype(F32)).astype(BF)
    near, head, far_h = after((near, head, far_h), third)
    up, down = send(third[:32], "z", 1), send(third[32:64], "z", -1)
    up_2 = send(third[64:], "z", 2)
    near_h = near[:cut] + head[cut:] + far_h.astype(F32)
    up = up.astype(F32) + up_2.astype(F32) + near_h[96:128]
    down = down.astype(F32) + near_h[128:]
    up, down = up.astype(BF), down.astype(BF)
    near_h, near_1 = after((near_h, near_h[32:96].astype(BF)), (up, pair))
    total = near_h[:32] + send(up, "z", 2).astype(F32) + send(down, "z", -2).astype(F32)
    total += send(near_1[:32], "z", 1).astype(F32) + send(near_1[32:], "z", -1).astype(F32)
    output, input_grad = total[:16].astype(BF), total[16:].astype(BF)
    grad_out = grad_out + pair[:h].astype(F32)
    grad_in_t = grad_in_t + pair[h:].astype(F32)
    return (output, input_grad, grad_in_t.T, grad_out)


def solution(mesh):
    mesh = Mesh(mesh.devices.reshape(8, 4, 4, 2), ("z", "x", "row", "col"))
    whole = ("z", "x", "col")
    placed = (P(whole, "row"), P("row", whole), P(whole, "row"), P(whole, "row"))
    return jax.shard_map(
        on_device,
        mesh=mesh,
        in_specs=placed,
        out_specs=(P(whole, "row"), P(whole, "row"), P("row", whole), P(whole, "row")),
        check_vma=False,
    )
```

```python
import jax
import jax.numpy as jnp
from jax import lax
from jax.experimental import pallas as pl
from jax.experimental.pallas import tpu as pltpu
from jax.sharding import Mesh, PartitionSpec as P

BF = jnp.bfloat16
F32 = jnp.float32
SIZE = {"z": 8, "x": 4, "row": 4, "col": 2}
ORDER = (0, 1, 7, 2, 6, 3, 5, 4)
HEAD = 5


def smooth_gate(value):
    return 0.5 * value * (1.0 + lax.erf(value * 0.7071067811865476))


def smooth_slope(value):
    cumul = 0.5 * (1.0 + lax.erf(value * 0.7071067811865476))
    return cumul + value * jnp.exp(-0.5 * value * value) * 0.3989422804014327


def send(value, axis, shift):
    size = SIZE[axis]
    return lax.ppermute(value, axis, [(i, (i + shift) % size) for i in range(size)])


def token_pair(value):
    return lax.ppermute(value, "x", [(0, 1), (1, 0), (2, 3), (3, 2)])


def weight_pair(value):
    return lax.ppermute(value, "x", [(0, 3), (3, 0), (1, 2), (2, 1)])


def after(value, other):
    return lax.optimization_barrier((value, other))[0]


def call(body, outs, args, flops=1 << 20, scratch=()):
    specs = [pl.BlockSpec(memory_space=pltpu.SMEM)]
    specs += [pl.BlockSpec(memory_space=pltpu.VMEM)] * (len(args) - 1)
    kernel = pl.pallas_call(
        body,
        out_shape=outs,
        in_specs=specs,
        out_specs=[pl.BlockSpec(memory_space=pltpu.VMEM)] * len(outs),
        scratch_shapes=list(scratch),
        compiler_params=pltpu.CompilerParams(vmem_limit_bytes=40 << 20),
        cost_estimate=pl.CostEstimate(
            flops=flops, bytes_accessed=1 << 20, transcendentals=0
        ),
    )
    return list(kernel(*args))


def cat(values):
    return jnp.concatenate(values, 0)


def dot(a, b, dim_a, dim_b):
    return lax.dot_general(
        a, b, (((dim_a,), (dim_b,)), ((), ())), preferred_element_type=F32
    )


def products(value_of, wi, wo, w_pair, part):
    h = wi.shape[0]
    for s, w in enumerate((wi, wo)):
        part[s, :h] = dot(w[...], value_of(s), 1, 1).astype(part.dtype)
        part[s, h:] = dot(w_pair[s * h : s * h + h], value_of(s), 1, 1).astype(part.dtype)


def quarter_of(tok, cot, index):
    rows = pl.ds(pl.multiple_of(index % 4 * 128, 128), 128)
    return lambda s: (tok, cot)[s][rows]


def up_kernel(me, *refs):
    quarters, (wi, wo, w_pair, tok, cot), parts = refs[:8], refs[8:13], refs[13:]
    for q in range(4):
        for j in range(8):
            ref, i = (quarters[2 * q], j) if j < HEAD else (quarters[2 * q + 1], j - HEAD)
            row = q * 128 + j * 16
            tok[row : row + 16] = ref[i * 32 : i * 32 + 16]
            cot[row : row + 16] = ref[i * 32 + 16 : i * 32 + 32]
    for k, part in zip((2, 1, 3), parts):
        products(quarter_of(tok, cot, me[0] + k), wi, wo, w_pair, part)


def mine_kernel(me, tok, cot, wi, wo, w_pair, part):
    products(quarter_of(tok, cot, me[0]), wi, wo, w_pair, part)


def act_kernel(me, p0, p1, p2, p3, out):
    del me
    pre, grad_act = p0[0], p0[1]
    for part in (p1, p2, p3):
        pre += part[0].astype(F32)
        grad_act += part[1].astype(F32)
    out[0] = smooth_gate(pre).astype(BF)
    out[1] = (grad_act * smooth_slope(pre)).astype(BF)


def down_kernel(me, full, wi, wo, w_pair, near, far, head, tail):
    del me
    h = wi.shape[0]
    for s, w in enumerate((wo, wi)):
        value = dot(full[s, :h], w[...], 0, 0)
        value += dot(full[s, h:], w_pair[(1 - s) * h : (2 - s) * h], 0, 0)
        for q in range(4):
            for j in range(8):
                piece = value[q * 128 + j * 16 : q * 128 + j * 16 + 16]
                row = j * 32 + s * 16
                if q < 2:
                    (near, far)[q][row : row + 16] = piece
                elif j < HEAD:
                    row += (3 - q) * HEAD * 32
                    head[row : row + 16] = piece.astype(BF)
                else:
                    row += (3 - q) * (8 - HEAD) * 32 - HEAD * 32
                    tail[row : row + 16] = piece.astype(BF)


def pair_kernel(me, b0, b2, b1, b3, tok, cot, full, out):
    h = full.shape[1] // 2
    for k, block in ((0, b0), (2, b2), (1, b1), (3, b3)):
        lane = pl.multiple_of(((me[0] + k) % 4) * 128, 128)
        full[:, :, pl.ds(lane, 128)] = block[...]
    out[:h] = dot(full[0, h:], cot[...], 1, 0).astype(BF)
    out[h:] = dot(full[1, h:], tok[...], 1, 0).astype(BF)


def own_kernel(me, full, tok, cot, grad_out, grad_in):
    del me
    h = full.shape[1] // 2
    grad_out[...] = dot(full[0, :h], cot[...], 1, 0)
    grad_in[...] = dot(full[1, :h], tok[...], 1, 0)


def on_device(tokens, w_in, w_out, cotangent):
    me = lax.axis_index("row").astype(jnp.int32).reshape(1)
    d, h = w_in.shape
    shape = jax.ShapeDtypeStruct
    flops = 2 * 1024 * d * h

    base = cat([tokens, cotangent])
    z = {0: base}
    z[2], z[6] = send(base, "z", -2), send(base, "z", 2)
    z[1], z[7] = send(base, "z", -1), send(base, "z", 1)
    w_in_t = w_in.T
    w_pair = weight_pair(after(cat([w_in_t, w_out]), base))
    z[3], z[5] = send(z[2], "z", -1), send(z[6], "z", 1)
    near_h = cat([z[k] for k in ORDER[:HEAD]])
    far_h = token_pair(near_h)
    z[4] = send(after(z[6], near_h), "z", 2)
    near_t = cat([z[k] for k in ORDER[HEAD:]])
    far_t = after(token_pair(near_t), w_pair)
    quarters = [near_h, near_t, far_h, far_t]
    quarters += [send(value, "col", 1) for value in quarters]

    part, rounded = shape((2, 2 * h, 128), F32), shape((2, 2 * h, 128), BF)
    weights = [w_in_t, w_out, w_pair]
    tok, cot, *parts = call(
        up_kernel, [shape((512, d), BF)] * 2 + [rounded] * 3, [me, *quarters, *weights], flops
    )
    mine = call(mine_kernel, [part], [me, after(tok, parts[0]), cot, *weights], flops)
    parts = mine + [send(value, "row", k) for k, value in zip((2, 1, 3), parts)]
    (block,) = call(act_kernel, [rounded], [me, *parts])
    blocks = [block] + [send(block, "row", -k) for k in (2, 1, 3)]

    sums = shape((256, d), F32)
    full, pair = call(
        pair_kernel,
        [shape((2, 2 * h, 512), BF), shape((2 * h, d), BF)],
        [me, *blocks, tok, cot],
        flops,
    )
    near, far, head, tail = call(
        down_kernel,
        [sums, sums, shape((HEAD * 64, d), BF), shape(((8 - HEAD) * 64, d), BF)],
        [me, full, w_in_t, w_out, w_pair],
        2 * flops,
    )
    cut, rest = HEAD * 32, (8 - HEAD) * 32
    tail = send(tail, "col", 1)
    head = send(after(head, tail), "col", 1).astype(F32)
    tail = tail.astype(F32)
    far_t = (far[cut:] + tail[:rest]).astype(BF)
    far = after(far, far_t)
    pair = weight_pair(after(pair, far_t))
    grad_out, grad_in_t = call(
        own_kernel, [shape((h, d), F32)] * 2, [me, full, after(tok, far_t), cot], flops
    )
    far_h = after((far[:cut] + head[:cut]).astype(BF), grad_out)
    far_t = after(token_pair(far_t), far_h)
    far_h = token_pair(far_h)
    third = (near[cut:] + tail[rest:] + far_t.astype(F32)).astype(BF)
    near, head, far_h = after((near, head, far_h), third)
    up, down = send(third[:32], "z", 1), send(third[32:64], "z", -1)
    up_2 = send(third[64:], "z", 2)
    near_h = near[:cut] + head[cut:] + far_h.astype(F32)
    up = up.astype(F32) + up_2.astype(F32) + near_h[96:128]
    down = down.astype(F32) + near_h[128:]
    up, down = up.astype(BF), down.astype(BF)
    near_h, near_1 = after((near_h, near_h[32:96].astype(BF)), (up, pair))
    total = near_h[:32] + send(up, "z", 2).astype(F32) + send(down, "z", -2).astype(F32)
    total += send(near_1[:32], "z", 1).astype(F32) + send(near_1[32:], "z", -1).astype(F32)
    output, input_grad = total[:16].astype(BF), total[16:].astype(BF)
    grad_out = grad_out + pair[:h].astype(F32)
    grad_in_t = grad_in_t + pair[h:].astype(F32)
    return (output, input_grad, grad_in_t.T, grad_out)


def solution(mesh):
    mesh = Mesh(mesh.devices.reshape(8, 4, 4, 2), ("z", "x", "row", "col"))
    whole = ("z", "x", "col")
    placed = (P(whole, "row"), P("row", whole), P(whole, "row"), P(whole, "row"))
    return jax.shard_map(
        on_device,
        mesh=mesh,
        in_specs=placed,
        out_specs=(P(whole, "row"), P(whole, "row"), P("row", whole), P(whole, "row")),
        check_vma=False,
    )
```

```python
import jax
import jax.numpy as jnp
from jax import lax
from jax.experimental import pallas as pl
from jax.experimental.pallas import tpu as pltpu
from jax.sharding import Mesh, PartitionSpec as P

BF = jnp.bfloat16
F32 = jnp.float32
SIZE = {"z": 8, "x": 4, "row": 4, "col": 2}
ORDER = (0, 1, 7, 2, 6, 3, 5, 4)
HEAD = 5


def smooth_gate(value):
    return 0.5 * value * (1.0 + lax.erf(value * 0.7071067811865476))


def smooth_slope(value):
    cumul = 0.5 * (1.0 + lax.erf(value * 0.7071067811865476))
    return cumul + value * jnp.exp(-0.5 * value * value) * 0.3989422804014327


def send(value, axis, shift):
    size = SIZE[axis]
    return lax.ppermute(value, axis, [(i, (i + shift) % size) for i in range(size)])


def token_pair(value):
    return lax.ppermute(value, "x", [(0, 1), (1, 0), (2, 3), (3, 2)])


def weight_pair(value):
    return lax.ppermute(value, "x", [(0, 3), (3, 0), (1, 2), (2, 1)])


def after(value, other):
    return lax.optimization_barrier((value, other))[0]


def call(body, outs, args, flops=1 << 20, scratch=()):
    specs = [pl.BlockSpec(memory_space=pltpu.SMEM)]
    specs += [pl.BlockSpec(memory_space=pltpu.VMEM)] * (len(args) - 1)
    kernel = pl.pallas_call(
        body,
        out_shape=outs,
        in_specs=specs,
        out_specs=[pl.BlockSpec(memory_space=pltpu.VMEM)] * len(outs),
        scratch_shapes=list(scratch),
        compiler_params=pltpu.CompilerParams(vmem_limit_bytes=40 << 20),
        cost_estimate=pl.CostEstimate(
            flops=flops, bytes_accessed=1 << 20, transcendentals=0
        ),
    )
    return list(kernel(*args))


def cat(values):
    return jnp.concatenate(values, 0)


def dot(a, b, dim_a, dim_b):
    return lax.dot_general(
        a, b, (((dim_a,), (dim_b,)), ((), ())), preferred_element_type=F32
    )


def products(value_of, wi, wo, w_pair, part):
    h = wi.shape[0]
    for s, w in enumerate((wi, wo)):
        part[s, :h] = dot(w[...], value_of(s), 1, 1).astype(part.dtype)
        part[s, h:] = dot(w_pair[s * h : s * h + h], value_of(s), 1, 1).astype(part.dtype)


def quarter_of(tok, cot, index):
    rows = pl.ds(pl.multiple_of(index % 4 * 128, 128), 128)
    return lambda s: (tok, cot)[s][rows]


def up_kernel(me, *refs):
    held, (wi, wo, w_pair, tok, cot), parts = refs[:8], refs[8:13], refs[13:]
    for q in range(4):
        half, chip = q // 2 * 4, q % 2
        for j in range(8):
            if j < 3:
                ref, i = held[half], j * 64 + chip * 32
            elif j < HEAD:
                ref, i = held[half + 1], chip * 64 + (j - 3) * 32
            else:
                ref, i = held[half + 2 + chip], (j - HEAD) * 32
            row = q * 128 + j * 16
            tok[row : row + 16] = ref[i : i + 16]
            cot[row : row + 16] = ref[i + 16 : i + 32]
    for k, part in zip((2, 1, 3), parts):
        products(quarter_of(tok, cot, me[0] + k), wi, wo, w_pair, part)


def mine_kernel(me, tok, cot, wi, wo, w_pair, part):
    products(quarter_of(tok, cot, me[0]), wi, wo, w_pair, part)


def act_kernel(me, p0, p1, p2, p3, out):
    del me
    pre, grad_act = p0[0], p0[1]
    for part in (p1, p2, p3):
        pre += part[0].astype(F32)
        grad_act += part[1].astype(F32)
    out[0] = smooth_gate(pre).astype(BF)
    out[1] = (grad_act * smooth_slope(pre)).astype(BF)


def down_kernel(me, full, wi, wo, w_pair, near, far, head, tail):
    del me
    h = wi.shape[0]
    for s, w in enumerate((wo, wi)):
        value = dot(full[s, :h], w[...], 0, 0)
        value += dot(full[s, h:], w_pair[(1 - s) * h : (2 - s) * h], 0, 0)
        for q in range(4):
            for j in range(8):
                piece = value[q * 128 + j * 16 : q * 128 + j * 16 + 16]
                row = j * 32 + s * 16
                if q < 2:
                    (near, far)[q][row : row + 16] = piece
                elif j < HEAD:
                    row += (3 - q) * HEAD * 32
                    head[row : row + 16] = piece.astype(BF)
                else:
                    row += (3 - q) * (8 - HEAD) * 32 - HEAD * 32
                    tail[row : row + 16] = piece.astype(BF)


def pair_kernel(me, b0, b2, b1, b3, tok, cot, full, out):
    h = full.shape[1] // 2
    for k, block in ((0, b0), (2, b2), (1, b1), (3, b3)):
        lane = pl.multiple_of(((me[0] + k) % 4) * 128, 128)
        full[:, :, pl.ds(lane, 128)] = block[...]
    out[:h] = dot(full[0, h:], cot[...], 1, 0).astype(BF)
    out[h:] = dot(full[1, h:], tok[...], 1, 0).astype(BF)


def own_kernel(me, full, tok, cot, grad_out, grad_in):
    del me
    h = full.shape[1] // 2
    grad_out[...] = dot(full[0, :h], cot[...], 1, 0)
    grad_in[...] = dot(full[1, :h], tok[...], 1, 0)


def on_device(tokens, w_in, w_out, cotangent):
    me = lax.axis_index("row").astype(jnp.int32).reshape(1)
    d, h = w_in.shape
    shape = jax.ShapeDtypeStruct
    flops = 2 * 1024 * d * h

    base = cat([tokens, cotangent])
    z = {2: send(base, "z", -2), 6: send(base, "z", 2)}
    both = cat([base, token_pair(base)])
    w_in_t = w_in.T
    w_pair = weight_pair(after(cat([w_in_t, w_out]), base))
    z[3], z[5] = send(z[2], "z", -1), send(z[6], "z", 1)
    second = cat([z[2], z[6]])
    z[4] = send(after(z[6], second), "z", 2)
    second = cat([second, token_pair(second)])
    near_t = cat([z[k] for k in ORDER[HEAD:]])
    both = after(both, z[3])
    first = cat([both, send(both, "z", -1), send(both, "z", 1)])
    far_t = after(token_pair(near_t), w_pair)
    held = [first, second, near_t, far_t]
    held += [send(value, "col", 1) for value in held]

    part, rounded = shape((2, 2 * h, 128), F32), shape((2, 2 * h, 128), BF)
    weights = [w_in_t, w_out, w_pair]
    tok, cot, *parts = call(
        up_kernel, [shape((512, d), BF)] * 2 + [rounded] * 3, [me, *held, *weights], flops
    )
    mine = call(mine_kernel, [part], [me, after(tok, parts[0]), cot, *weights], flops)
    parts = mine + [send(value, "row", k) for k, value in zip((2, 1, 3), parts)]
    (block,) = call(act_kernel, [rounded], [me, *parts])
    blocks = [block] + [send(block, "row", -k) for k in (2, 1, 3)]

    sums = shape((256, d), F32)
    full, pair = call(
        pair_kernel,
        [shape((2, 2 * h, 512), BF), shape((2 * h, d), BF)],
        [me, *blocks, tok, cot],
        flops,
    )
    near, far, head, tail = call(
        down_kernel,
        [sums, sums, shape((HEAD * 64, d), BF), shape(((8 - HEAD) * 64, d), BF)],
        [me, full, w_in_t, w_out, w_pair],
        2 * flops,
    )
    cut, rest = HEAD * 32, (8 - HEAD) * 32
    tail = send(tail, "col", 1)
    head = send(after(head, tail), "col", 1).astype(F32)
    tail = tail.astype(F32)
    far_t = (far[cut:] + tail[:rest]).astype(BF)
    far = after(far, far_t)
    pair = weight_pair(after(pair, far_t))
    grad_out, grad_in_t = call(
        own_kernel, [shape((h, d), F32)] * 2, [me, full, after(tok, far_t), cot], flops
    )
    far_t = token_pair(far_t)
    head = after(head, grad_out)
    far_h = far[:cut] + head[:cut]
    near_h = near[:cut] + head[cut:]
    up_1 = cat([near_h[32:64], far_h[32:64]]).astype(BF)
    down_1 = cat([near_h[64:96], far_h[64:96]]).astype(BF)
    near = after(near, (up_1, down_1))
    up_1, down_1 = send(up_1, "z", 1).astype(F32), send(down_1, "z", -1).astype(F32)
    far_2 = token_pair(far_h[96:].astype(BF)).astype(F32)
    third = (near[cut:] + tail[rest:] + far_t.astype(F32)).astype(BF)
    up, down = send(third[:32], "z", 1), send(third[32:64], "z", -1)
    up_2 = send(third[64:], "z", 2)
    far_0 = after(far_h[:32], third) + up_1[32:] + down_1[32:]
    far_0 = token_pair(far_0.astype(BF)).astype(F32)
    near_2 = after(near_h[96:], far_0)
    up = (up.astype(F32) + up_2.astype(F32) + near_2[:32] + far_2[:32]).astype(BF)
    down = (down.astype(F32) + near_2[32:] + far_2[32:]).astype(BF)
    total = after(near_h[:32], up) + up_1[:32] + down_1[:32] + far_0
    total += send(up, "z", 2).astype(F32) + send(down, "z", -2).astype(F32)
    output, input_grad = total[:16].astype(BF), total[16:].astype(BF)
    grad_out = grad_out + pair[:h].astype(F32)
    grad_in_t = grad_in_t + pair[h:].astype(F32)
    return (output, input_grad, grad_in_t.T, grad_out)


def solution(mesh):
    mesh = Mesh(mesh.devices.reshape(8, 4, 4, 2), ("z", "x", "row", "col"))
    whole = ("z", "x", "col")
    placed = (P(whole, "row"), P("row", whole), P(whole, "row"), P(whole, "row"))
    return jax.shard_map(
        on_device,
        mesh=mesh,
        in_specs=placed,
        out_specs=(P(whole, "row"), P(whole, "row"), P("row", whole), P(whole, "row")),
        check_vma=False,
    )
```

```python
import jax
import jax.numpy as jnp
from jax import lax
from jax.experimental import pallas as pl
from jax.experimental.pallas import tpu as pltpu
from jax.sharding import Mesh, PartitionSpec as P

BF = jnp.bfloat16
F32 = jnp.float32
SIZE = {"z": 8, "x": 4, "row": 4, "col": 2}
ORDER = (0, 1, 7, 2, 6, 3, 5, 4)
HEAD = 5


def smooth_gate(value):
    return 0.5 * value * (1.0 + lax.erf(value * 0.7071067811865476))


def smooth_slope(value):
    cumul = 0.5 * (1.0 + lax.erf(value * 0.7071067811865476))
    return cumul + value * jnp.exp(-0.5 * value * value) * 0.3989422804014327


def send(value, axis, shift):
    size = SIZE[axis]
    return lax.ppermute(value, axis, [(i, (i + shift) % size) for i in range(size)])


def token_pair(value):
    return lax.ppermute(value, "x", [(0, 1), (1, 0), (2, 3), (3, 2)])


def weight_pair(value):
    return lax.ppermute(value, "x", [(0, 3), (3, 0), (1, 2), (2, 1)])


def after(value, other):
    return lax.optimization_barrier((value, other))[0]


def call(body, outs, args, flops=1 << 20, scratch=(), aliases=None):
    specs = [pl.BlockSpec(memory_space=pltpu.SMEM)]
    specs += [pl.BlockSpec(memory_space=pltpu.VMEM)] * (len(args) - 1)
    kernel = pl.pallas_call(
        body,
        out_shape=outs,
        in_specs=specs,
        out_specs=[pl.BlockSpec(memory_space=pltpu.VMEM)] * len(outs),
        scratch_shapes=list(scratch),
        input_output_aliases=aliases or {},
        compiler_params=pltpu.CompilerParams(vmem_limit_bytes=40 << 20),
        cost_estimate=pl.CostEstimate(
            flops=flops, bytes_accessed=1 << 20, transcendentals=0
        ),
    )
    return list(kernel(*args))


def cat(values):
    return jnp.concatenate(values, 0)


def dot(a, b, dim_a, dim_b):
    return lax.dot_general(
        a, b, (((dim_a,), (dim_b,)), ((), ())), preferred_element_type=F32
    )


def products(value_of, wi, wo, w_pair, part):
    h = wi.shape[0]
    for s, w in enumerate((wi, wo)):
        part[s, :h] = dot(w[...], value_of(s), 1, 1).astype(part.dtype)
        part[s, h:] = dot(w_pair[s * h : s * h + h], value_of(s), 1, 1).astype(part.dtype)


def order_tokens(q, held, slots, tok, cot):
    first, second, third = held
    chip = q % 2
    for j in slots:
        if j < 3:
            ref, i = first, j * 64 + chip * 32
        elif j < HEAD:
            ref, i = second, chip * 64 + (j - 3) * 32
        else:
            ref, i = third, (j - HEAD) * 32
        row = q * 128 + j * 16
        tok[row : row + 16] = ref[i : i + 16]
        cot[row : row + 16] = ref[i + 16 : i + 32]


def up_kernel(me, a0, a1, a2, a3, b0, b1, b2, wi, wo, w_pair, tok, cot, whole):
    del me
    order_tokens(0, (a0, a1, a2), range(8), tok, cot)
    order_tokens(1, (a0, a1, a3), range(8), tok, cot)
    order_tokens(2, (b0, b1, b2), range(8), tok, cot)
    order_tokens(3, (b0, b1, None), range(HEAD), tok, cot)
    for q in range(3):
        rows = slice(q * 128, q * 128 + 128)
        products(lambda s: (tok, cot)[s][rows], wi, wo, w_pair, whole.at[q])


def last_kernel(me, tok_in, cot_in, b3, wi, wo, w_pair, three, tok, cot, p0, p2, p1, p3, whole):
    del tok_in, cot_in
    order_tokens(3, (None, None, b3), range(HEAD, 8), tok, cot)
    whole[:3] = three[...]
    products(lambda s: (tok, cot)[s][384:], wi, wo, w_pair, whole.at[3])
    for k, part in ((2, p2), (1, p1), (3, p3), (0, p0)):
        part[...] = whole[(me[0] + k) % 4].astype(part.dtype)


def act_kernel(me, p0, p1, p2, p3, out):
    del me
    pre, grad_act = p0[0], p0[1]
    for part in (p1, p2, p3):
        pre += part[0].astype(F32)
        grad_act += part[1].astype(F32)
    out[0] = smooth_gate(pre).astype(BF)
    out[1] = (grad_act * smooth_slope(pre)).astype(BF)


def down_kernel(me, c0, c2, c1, c3, wi, wo, w_pair, near, far, head, tail, full):
    for k, block in ((0, c0), (2, c2), (1, c1), (3, c3)):
        lane = pl.multiple_of(((me[0] + k) % 4) * 128, 128)
        full[:, :, pl.ds(lane, 128)] = block[...]
    h = wi.shape[0]
    for s, w in enumerate((wo, wi)):
        value = dot(full[s, :h], w[...], 0, 0)
        value += dot(full[s, h:], w_pair[(1 - s) * h : (2 - s) * h], 0, 0)
        for q in range(4):
            for j in range(8):
                piece = value[q * 128 + j * 16 : q * 128 + j * 16 + 16]
                row = j * 32 + s * 16
                if q < 2:
                    (near, far)[q][row : row + 16] = piece
                elif j < HEAD:
                    row += (3 - q) * HEAD * 32
                    head[row : row + 16] = piece.astype(BF)
                else:
                    row += (3 - q) * (8 - HEAD) * 32 - HEAD * 32
                    tail[row : row + 16] = piece.astype(BF)


def pair_kernel(me, full, tok, cot, out):
    del me
    h = full.shape[1] // 2
    out[:h] = dot(full[0, h:], cot[...], 1, 0).astype(BF)
    out[h:] = dot(full[1, h:], tok[...], 1, 0).astype(BF)


def own_kernel(me, full, tok, cot, grad_out, grad_in):
    del me
    h = full.shape[1] // 2
    grad_out[...] = dot(full[0, :h], cot[...], 1, 0)
    grad_in[...] = dot(full[1, :h], tok[...], 1, 0)


def on_device(tokens, w_in, w_out, cotangent):
    me = lax.axis_index("row").astype(jnp.int32).reshape(1)
    d, h = w_in.shape
    shape = jax.ShapeDtypeStruct
    flops = 2 * 1024 * d * h

    base = cat([tokens, cotangent])
    z = {2: send(base, "z", -2), 6: send(base, "z", 2)}
    both = cat([base, token_pair(base)])
    w_in_t = w_in.T
    w_pair = weight_pair(after(cat([w_in_t, w_out]), base))
    z[3], z[5] = send(z[2], "z", -1), send(z[6], "z", 1)
    second = cat([z[2], z[6]])
    z[4] = send(after(z[6], second), "z", 2)
    second = cat([second, token_pair(second)])
    near_t = cat([z[k] for k in ORDER[HEAD:]])
    both = after(both, z[3])
    first = cat([both, send(both, "z", -1), send(both, "z", 1)])
    far_t = after(token_pair(near_t), w_pair)
    held = [first, second, near_t, far_t]
    held += [send(value, "col", 1) for value in held]

    part, rounded = shape((2, 2 * h, 128), F32), shape((2, 2 * h, 128), BF)
    weights = [w_in_t, w_out, w_pair]
    tokens_all = [shape((512, d), BF)] * 2
    tok, cot, three = call(
        up_kernel, tokens_all + [shape((3, *part.shape), F32)], [me, *held[:7], *weights], flops
    )
    tok, cot, *parts = call(
        last_kernel,
        tokens_all + [part] + [rounded] * 3,
        [me, tok, cot, held[7], *weights, three],
        flops,
        [pltpu.VMEM((4, *part.shape), F32)],
        {1: 0, 2: 1},
    )
    parts[1:] = [send(value, "row", k) for k, value in zip((2, 1, 3), parts[1:])]
    (block,) = call(act_kernel, [rounded], [me, *parts])
    blocks = [block] + [send(block, "row", -k) for k in (2, 1, 3)]

    sums = shape((256, d), F32)
    near, far, head, tail, full = call(
        down_kernel,
        [sums, sums, shape((HEAD * 64, d), BF), shape(((8 - HEAD) * 64, d), BF), shape((2, 2 * h, 512), BF)],
        [me, *blocks, w_in_t, w_out, w_pair],
        2 * flops,
    )
    cut, rest = HEAD * 32, (8 - HEAD) * 32
    tail = send(tail, "col", 1)
    head = send(after(head, tail), "col", 1).astype(F32)
    tail = tail.astype(F32)
    far_t = (far[cut:] + tail[:rest]).astype(BF)
    far = after(far, far_t)
    (pair,) = call(
        pair_kernel, [shape((2 * h, d), BF)], [me, after(full, far_t), tok, cot], flops
    )
    pair = weight_pair(pair)
    grad_out, grad_in_t = call(
        own_kernel, [shape((h, d), F32)] * 2, [me, full, after(tok, far_t), cot], flops
    )
    head = after(head, grad_out)
    far_h = far[:cut] + head[:cut]
    near_h = near[:cut] + head[cut:]
    up_1 = cat([near_h[32:64], far_h[32:64]]).astype(BF)
    down_1 = cat([near_h[64:96], far_h[64:96]]).astype(BF)
    near = after(near, (up_1, down_1))
    up_1, down_1 = send(up_1, "z", 1).astype(F32), send(down_1, "z", -1).astype(F32)
    far_2 = far_h[96:].astype(BF)
    far_t = after(token_pair(far_t), far_2)
    far_2 = token_pair(far_2).astype(F32)
    third = (near[cut:] + tail[rest:] + far_t.astype(F32)).astype(BF)
    up, down = send(third[:32], "z", 1), send(third[32:64], "z", -1)
    up_2 = send(third[64:], "z", 2)
    far_0 = after(far_h[:32], third) + up_1[32:] + down_1[32:]
    far_0 = token_pair(far_0.astype(BF)).astype(F32)
    near_2 = after(near_h[96:], far_0)
    up = (up.astype(F32) + up_2.astype(F32) + near_2[:32] + far_2[:32]).astype(BF)
    down = (down.astype(F32) + near_2[32:] + far_2[32:]).astype(BF)
    total = after(near_h[:32], up) + up_1[:32] + down_1[:32] + far_0
    total += send(up, "z", 2).astype(F32) + send(down, "z", -2).astype(F32)
    output, input_grad = total[:16].astype(BF), total[16:].astype(BF)
    grad_out = grad_out + pair[:h].astype(F32)
    grad_in_t = grad_in_t + pair[h:].astype(F32)
    return (output, input_grad, grad_in_t.T, grad_out)


def solution(mesh):
    mesh = Mesh(mesh.devices.reshape(8, 4, 4, 2), ("z", "x", "row", "col"))
    whole = ("z", "x", "col")
    placed = (P(whole, "row"), P("row", whole), P(whole, "row"), P(whole, "row"))
    return jax.shard_map(
        on_device,
        mesh=mesh,
        in_specs=placed,
        out_specs=(P(whole, "row"), P(whole, "row"), P("row", whole), P(whole, "row")),
        check_vma=False,
    )
```

```python
import jax
import jax.numpy as jnp
from jax import lax
from jax.experimental import pallas as pl
from jax.experimental.pallas import tpu as pltpu
from jax.sharding import Mesh, PartitionSpec as P

BF = jnp.bfloat16
F32 = jnp.float32
SIZE = {"z": 8, "x": 4, "row": 4, "col": 2}
ORDER = (0, 1, 7, 2, 6, 3, 5, 4)
HEAD = 5


def smooth_gate(value):
    return 0.5 * value * (1.0 + lax.erf(value * 0.7071067811865476))


def smooth_slope(value):
    cumul = 0.5 * (1.0 + lax.erf(value * 0.7071067811865476))
    return cumul + value * jnp.exp(-0.5 * value * value) * 0.3989422804014327


def send(value, axis, shift):
    size = SIZE[axis]
    return lax.ppermute(value, axis, [(i, (i + shift) % size) for i in range(size)])


def token_pair(value):
    return lax.ppermute(value, "x", [(0, 1), (1, 0), (2, 3), (3, 2)])


def weight_pair(value):
    return lax.ppermute(value, "x", [(0, 3), (3, 0), (1, 2), (2, 1)])


def after(value, other):
    return lax.optimization_barrier((value, other))[0]


def call(body, outs, args, flops=1 << 20, scratch=()):
    specs = [pl.BlockSpec(memory_space=pltpu.SMEM)]
    specs += [pl.BlockSpec(memory_space=pltpu.VMEM)] * (len(args) - 1)
    kernel = pl.pallas_call(
        body,
        out_shape=outs,
        in_specs=specs,
        out_specs=[pl.BlockSpec(memory_space=pltpu.VMEM)] * len(outs),
        scratch_shapes=list(scratch),
        compiler_params=pltpu.CompilerParams(vmem_limit_bytes=40 << 20),
        cost_estimate=pl.CostEstimate(
            flops=flops, bytes_accessed=1 << 20, transcendentals=0
        ),
    )
    return list(kernel(*args))


def cat(values):
    return jnp.concatenate(values, 0)


def dot(a, b, dim_a, dim_b):
    return lax.dot_general(
        a, b, (((dim_a,), (dim_b,)), ((), ())), preferred_element_type=F32
    )


def products(value_of, wi, wo, w_pair, part):
    h = wi.shape[0]
    for s, w in enumerate((wi, wo)):
        part[s, :h] = dot(w[...], value_of(s), 1, 1).astype(part.dtype)
        part[s, h:] = dot(w_pair[s * h : s * h + h], value_of(s), 1, 1).astype(part.dtype)


def quarter_of(tok, cot, index):
    rows = pl.ds(pl.multiple_of(index % 4 * 128, 128), 128)
    return lambda s: (tok, cot)[s][rows]


def up_kernel(me, *refs):
    held, (wi, wo, w_pair, tok, cot), parts = refs[:8], refs[8:13], refs[13:]
    for q in range(4):
        first, second, third, fourth = held[q // 2 * 4 : q // 2 * 4 + 4]
        chip = q % 2
        for j in range(8):
            if j < 3:
                ref, i = first, j * 64 + chip * 32
            elif j < 5:
                ref, i = second, chip * 64 + (j - 3) * 32
            elif j < 7:
                ref, i = third, chip * 64 + (j - 5) * 32
            else:
                ref, i = fourth, chip * 32
            row = q * 128 + j * 16
            tok[row : row + 16] = ref[i : i + 16]
            cot[row : row + 16] = ref[i + 16 : i + 32]
    for k, part in zip((2, 1, 3), parts):
        products(quarter_of(tok, cot, me[0] + k), wi, wo, w_pair, part)


def mine_kernel(me, tok, cot, wi, wo, w_pair, part):
    products(quarter_of(tok, cot, me[0]), wi, wo, w_pair, part)


def act_kernel(me, p0, p1, p2, p3, out):
    del me
    pre, grad_act = p0[0], p0[1]
    for part in (p1, p2, p3):
        pre += part[0].astype(F32)
        grad_act += part[1].astype(F32)
    out[0] = smooth_gate(pre).astype(BF)
    out[1] = (grad_act * smooth_slope(pre)).astype(BF)


def down_kernel(me, c0, c2, c1, c3, wi, wo, w_pair, near, far, head, tail, full):
    for k, block in ((0, c0), (2, c2), (1, c1), (3, c3)):
        lane = pl.multiple_of(((me[0] + k) % 4) * 128, 128)
        full[:, :, pl.ds(lane, 128)] = block[...]
    h = wi.shape[0]
    for s, w in enumerate((wo, wi)):
        value = dot(full[s, :h], w[...], 0, 0)
        value += dot(full[s, h:], w_pair[(1 - s) * h : (2 - s) * h], 0, 0)
        for q in range(4):
            for j in range(8):
                piece = value[q * 128 + j * 16 : q * 128 + j * 16 + 16]
                row = j * 32 + s * 16
                if q < 2:
                    (near, far)[q][row : row + 16] = piece
                elif j < HEAD:
                    row += (3 - q) * HEAD * 32
                    head[row : row + 16] = piece.astype(BF)
                else:
                    row += (3 - q) * (8 - HEAD) * 32 - HEAD * 32
                    tail[row : row + 16] = piece.astype(BF)


def pair_kernel(me, full, tok, cot, out):
    del me
    h = full.shape[1] // 2
    out[:h] = dot(full[0, h:], cot[...], 1, 0).astype(BF)
    out[h:] = dot(full[1, h:], tok[...], 1, 0).astype(BF)


def own_kernel(me, full, tok, cot, grad_out, grad_in):
    del me
    h = full.shape[1] // 2
    grad_out[...] = dot(full[0, :h], cot[...], 1, 0)
    grad_in[...] = dot(full[1, :h], tok[...], 1, 0)


def on_device(tokens, w_in, w_out, cotangent):
    me = lax.axis_index("row").astype(jnp.int32).reshape(1)
    d, h = w_in.shape
    shape = jax.ShapeDtypeStruct
    flops = 2 * 1024 * d * h

    base = cat([tokens, cotangent])
    z = {2: send(base, "z", -2), 6: send(base, "z", 2)}
    both = cat([base, token_pair(base)])
    w_in_t = w_in.T
    w_pair = weight_pair(after(cat([w_in_t, w_out]), base))
    z[3], z[5] = send(z[2], "z", -1), send(z[6], "z", 1)
    second = cat([z[2], z[6]])
    second = cat([second, token_pair(second)])
    fourth = cat([second[32:64], second[96:]])
    both = after(both, (fourth, z[3]))
    fourth = send(fourth, "z", 2)
    third = cat([z[3], z[5]])
    first = cat([both, send(both, "z", -1), send(both, "z", 1)])
    third = cat([third, after(token_pair(third), w_pair)])
    held = [first, second, third, fourth]
    held += [send(value, "col", 1) for value in held]

    part, rounded = shape((2, 2 * h, 128), F32), shape((2, 2 * h, 128), BF)
    weights = [w_in_t, w_out, w_pair]
    tok, cot, *parts = call(
        up_kernel, [shape((512, d), BF)] * 2 + [rounded] * 3, [me, *held, *weights], flops
    )
    mine = call(mine_kernel, [part], [me, after(tok, parts[0]), cot, *weights], flops)
    parts = mine + [send(value, "row", k) for k, value in zip((2, 1, 3), parts)]
    (block,) = call(act_kernel, [rounded], [me, *parts])
    blocks = [block] + [send(block, "row", -k) for k in (2, 1, 3)]

    sums = shape((256, d), F32)
    near, far, head, tail, full = call(
        down_kernel,
        [sums, sums, shape((HEAD * 64, d), BF), shape(((8 - HEAD) * 64, d), BF), shape((2, 2 * h, 512), BF)],
        [me, *blocks, w_in_t, w_out, w_pair],
        2 * flops,
    )
    cut, rest = HEAD * 32, (8 - HEAD) * 32
    tail = send(tail, "col", 1)
    head = send(after(head, tail), "col", 1).astype(F32)
    tail = tail.astype(F32)
    far_t = far[cut:] + tail[:rest]
    near_t = near[cut:] + tail[rest:]
    fourth = cat([near_t[64:], far_t[64:]]).astype(BF)
    far_t = far_t[:64].astype(BF)
    near, far = after((near, far), far_t)
    (pair,) = call(
        pair_kernel, [shape((2 * h, d), BF)], [me, after(full, far_t), tok, cot], flops
    )
    pair = weight_pair(pair)
    grad_out, grad_in_t = call(
        own_kernel, [shape((h, d), F32)] * 2, [me, full, after(tok, far_t), cot], flops
    )
    fourth = send(fourth, "z", 2).astype(F32)
    head = after(head, grad_out)
    far_h = far[:cut] + head[:cut]
    near_h = near[:cut] + head[cut:]
    up_1 = cat([near_h[32:64], far_h[32:64]]).astype(BF)
    down_1 = cat([near_h[64:96], far_h[64:96]]).astype(BF)
    near_t = after(near_t, (up_1, down_1))
    up_1, down_1 = send(up_1, "z", 1).astype(F32), send(down_1, "z", -1).astype(F32)
    third = (near_t[:64] + token_pair(far_t).astype(F32)).astype(BF)
    up, down = send(third[:32], "z", 1), send(third[32:], "z", -1)
    far_2, near_2 = after((far_h[96:], near_h[96:]), third)
    far_2 = cat([far_2[:32] + fourth[32:], far_2[32:]]).astype(BF)
    far_2 = token_pair(far_2).astype(F32)
    far_0 = after(far_h[:32], third) + up_1[32:] + down_1[32:]
    far_0 = token_pair(far_0.astype(BF)).astype(F32)
    near_2 = after(near_2, far_0)
    up = (up.astype(F32) + fourth[:32] + near_2[:32] + far_2[:32]).astype(BF)
    down = (down.astype(F32) + near_2[32:] + far_2[32:]).astype(BF)
    total = after(near_h[:32], up) + up_1[:32] + down_1[:32] + far_0
    total += send(up, "z", 2).astype(F32) + send(down, "z", -2).astype(F32)
    output, input_grad = total[:16].astype(BF), total[16:].astype(BF)
    grad_out = grad_out + pair[:h].astype(F32)
    grad_in_t = grad_in_t + pair[h:].astype(F32)
    return (output, input_grad, grad_in_t.T, grad_out)


def solution(mesh):
    mesh = Mesh(mesh.devices.reshape(8, 4, 4, 2), ("z", "x", "row", "col"))
    whole = ("z", "x", "col")
    placed = (P(whole, "row"), P("row", whole), P(whole, "row"), P(whole, "row"))
    return jax.shard_map(
        on_device,
        mesh=mesh,
        in_specs=placed,
        out_specs=(P(whole, "row"), P(whole, "row"), P("row", whole), P(whole, "row")),
        check_vma=False,
    )
```

```python
import jax
import jax.numpy as jnp
from jax import lax
from jax.experimental import pallas as pl
from jax.experimental.pallas import tpu as pltpu
from jax.sharding import Mesh, PartitionSpec as P

BF = jnp.bfloat16
F32 = jnp.float32
SIZE = {"z": 8, "x": 4, "row": 4, "col": 2}
ORDER = (0, 1, 7, 2, 6, 3, 5, 4)
HEAD = 5


def smooth_gate(value):
    return 0.5 * value * (1.0 + lax.erf(value * 0.7071067811865476))


def smooth_slope(value):
    cumul = 0.5 * (1.0 + lax.erf(value * 0.7071067811865476))
    return cumul + value * jnp.exp(-0.5 * value * value) * 0.3989422804014327


def send(value, axis, shift):
    size = SIZE[axis]
    return lax.ppermute(value, axis, [(i, (i + shift) % size) for i in range(size)])


def token_pair(value):
    return lax.ppermute(value, "x", [(0, 1), (1, 0), (2, 3), (3, 2)])


def weight_pair(value):
    return lax.ppermute(value, "x", [(0, 3), (3, 0), (1, 2), (2, 1)])


def after(value, other):
    return lax.optimization_barrier((value, other))[0]


def call(body, outs, args, flops=1 << 20, scratch=()):
    specs = [pl.BlockSpec(memory_space=pltpu.SMEM)]
    specs += [pl.BlockSpec(memory_space=pltpu.VMEM)] * (len(args) - 1)
    kernel = pl.pallas_call(
        body,
        out_shape=outs,
        in_specs=specs,
        out_specs=[pl.BlockSpec(memory_space=pltpu.VMEM)] * len(outs),
        scratch_shapes=list(scratch),
        compiler_params=pltpu.CompilerParams(vmem_limit_bytes=40 << 20),
        cost_estimate=pl.CostEstimate(
            flops=flops, bytes_accessed=1 << 20, transcendentals=0
        ),
    )
    return list(kernel(*args))


def cat(values):
    return jnp.concatenate(values, 0)


def dot(a, b, dim_a, dim_b):
    return lax.dot_general(
        a, b, (((dim_a,), (dim_b,)), ((), ())), preferred_element_type=F32
    )


def products(value_of, wi, wo, w_pair, part):
    h = wi.shape[0]
    for s, w in enumerate((wi, wo)):
        part[s, :h] = dot(w[...], value_of(s), 1, 1).astype(part.dtype)
        part[s, h:] = dot(w_pair[s * h : s * h + h], value_of(s), 1, 1).astype(part.dtype)


def quarter_of(tok, cot, index):
    rows = pl.ds(pl.multiple_of(index % 4 * 128, 128), 128)
    return lambda s: (tok, cot)[s][rows]


def up_kernel(me, *refs):
    held, (wi, wo, w_pair, tok, cot), parts = refs[:8], refs[8:13], refs[13:]
    for q in range(4):
        half, chip = q // 2 * 4, q % 2
        for j in range(8):
            if j < 3:
                ref, i = held[half], j * 64 + chip * 32
            elif j < HEAD:
                ref, i = held[half + 1], chip * 64 + (j - 3) * 32
            else:
                ref, i = held[half + 2 + chip], (j - HEAD) * 32
            row = q * 128 + j * 16
            tok[row : row + 16] = ref[i : i + 16]
            cot[row : row + 16] = ref[i + 16 : i + 32]
    for k, part in zip((2, 1, 3), parts):
        products(quarter_of(tok, cot, me[0] + k), wi, wo, w_pair, part)


def mine_kernel(me, tok, cot, wi, wo, w_pair, part):
    products(quarter_of(tok, cot, me[0]), wi, wo, w_pair, part)


def act_kernel(me, p0, p1, p2, p3, out):
    del me
    pre, grad_act = p0[0], p0[1]
    for part in (p1, p2, p3):
        pre += part[0].astype(F32)
        grad_act += part[1].astype(F32)
    out[0] = smooth_gate(pre).astype(BF)
    out[1] = (grad_act * smooth_slope(pre)).astype(BF)


def down_kernel(me, c0, c2, c1, c3, wi, wo, w_pair, near, far, head, tail, full):
    for k, block in ((0, c0), (2, c2), (1, c1), (3, c3)):
        lane = pl.multiple_of(((me[0] + k) % 4) * 128, 128)
        full[:, :, pl.ds(lane, 128)] = block[...]
    h = wi.shape[0]
    for s, w in enumerate((wo, wi)):
        value = dot(full[s, :h], w[...], 0, 0)
        value += dot(full[s, h:], w_pair[(1 - s) * h : (2 - s) * h], 0, 0)
        for q in range(4):
            for j in range(8):
                piece = value[q * 128 + j * 16 : q * 128 + j * 16 + 16]
                row = j * 32 + s * 16
                if q < 2:
                    (near, far)[q][row : row + 16] = piece
                elif j < HEAD:
                    row += (4 - q) * HEAD * 32 - (2 * HEAD - 8) * 32
                    head[row : row + 16] = piece.astype(BF)
                else:
                    row -= HEAD * 32
                    (head, tail)[q - 2][row : row + 16] = piece.astype(BF)


def pair_kernel(me, full, tok, cot, out):
    del me
    h = full.shape[1] // 2
    out[:h] = dot(full[0, h:], cot[...], 1, 0).astype(BF)
    out[h:] = dot(full[1, h:], tok[...], 1, 0).astype(BF)


def own_kernel(me, full, tok, cot, grad_out, grad_in):
    del me
    h = full.shape[1] // 2
    grad_out[...] = dot(full[0, :h], cot[...], 1, 0)
    grad_in[...] = dot(full[1, :h], tok[...], 1, 0)


def on_device(tokens, w_in, w_out, cotangent):
    me = lax.axis_index("row").astype(jnp.int32).reshape(1)
    d, h = w_in.shape
    shape = jax.ShapeDtypeStruct
    flops = 2 * 1024 * d * h

    base = cat([tokens, cotangent])
    z = {2: send(base, "z", -2), 6: send(base, "z", 2)}
    both = cat([base, token_pair(base)])
    w_in_t = w_in.T
    w_pair = weight_pair(after(cat([w_in_t, w_out]), base))
    z[3], z[5] = send(z[2], "z", -1), send(z[6], "z", 1)
    second = cat([z[2], z[6]])
    z[4] = send(after(z[6], second), "z", 2)
    second = cat([second, token_pair(second)])
    near_t = cat([z[k] for k in ORDER[HEAD:]])
    both = after(both, z[3])
    first = cat([both, send(both, "z", -1), send(both, "z", 1)])
    far_t = after(token_pair(near_t), w_pair)
    held = [first, second, near_t, far_t]
    held += [send(value, "col", 1) for value in held]

    part, rounded = shape((2, 2 * h, 128), F32), shape((2, 2 * h, 128), BF)
    weights = [w_in_t, w_out, w_pair]
    tok, cot, *parts = call(
        up_kernel, [shape((512, d), BF)] * 2 + [rounded] * 3, [me, *held, *weights], flops
    )
    mine = call(mine_kernel, [part], [me, after(tok, parts[0]), cot, *weights], flops)
    parts[1:] = after(tuple(parts[1:]), mine[0])
    parts = mine + [send(value, "row", k) for k, value in zip((2, 1, 3), parts)]
    (block,) = call(act_kernel, [rounded], [me, *parts])
    blocks = [block] + [send(block, "row", -k) for k in (2, 1, 3)]

    sums = shape((256, d), F32)
    near, far, head, tail, full = call(
        down_kernel,
        [sums, sums, shape((256 + HEAD * 32, d), BF), shape((256 - HEAD * 32, d), BF), shape((2, 2 * h, 512), BF)],
        [me, *blocks, w_in_t, w_out, w_pair],
        2 * flops,
    )
    cut, rest = HEAD * 32, (8 - HEAD) * 32
    tail = send(tail, "col", 1)
    head = send(after(head, tail), "col", 1).astype(F32)
    far_t = (far[cut:] + tail.astype(F32)).astype(BF)
    far = after(far, far_t)
    (pair,) = call(
        pair_kernel, [shape((2 * h, d), BF)], [me, after(full, far_t), tok, cot], flops
    )
    pair = weight_pair(pair)
    grad_out, grad_in_t = call(
        own_kernel, [shape((h, d), F32)] * 2, [me, full, after(tok, far_t), cot], flops
    )
    head = after(head, grad_out)
    far_h = far[:cut] + head[rest:256]
    near_h = near[:cut] + head[256:]
    up_1 = cat([near_h[32:64], far_h[32:64]]).astype(BF)
    down_1 = cat([near_h[64:96], far_h[64:96]]).astype(BF)
    near, head = after((near, head), (up_1, down_1))
    up_1, down_1 = send(up_1, "z", 1).astype(F32), send(down_1, "z", -1).astype(F32)
    far_2 = far_h[96:].astype(BF)
    far_t = after(token_pair(far_t), far_2)
    far_2 = token_pair(far_2).astype(F32)
    third = (near[cut:] + head[:rest] + far_t.astype(F32)).astype(BF)
    up_2 = send(third[64:], "z", 2)
    up, down = send(third[:32], "z", 1), send(third[32:64], "z", -1)
    far_0 = after(far_h[:32], third) + up_1[32:] + down_1[32:]
    far_0 = token_pair(far_0.astype(BF)).astype(F32)
    near_2 = after(near_h[96:], far_0)
    up = (up_2.astype(F32) + up.astype(F32) + near_2[:32] + far_2[:32]).astype(BF)
    down = (down.astype(F32) + near_2[32:] + far_2[32:]).astype(BF)
    total = after(near_h[:32], up) + up_1[:32] + down_1[:32] + far_0
    total += send(up, "z", 2).astype(F32) + send(down, "z", -2).astype(F32)
    output, input_grad = total[:16].astype(BF), total[16:].astype(BF)
    grad_out = grad_out + pair[:h].astype(F32)
    grad_in_t = grad_in_t + pair[h:].astype(F32)
    return (output, input_grad, grad_in_t.T, grad_out)


def solution(mesh):
    mesh = Mesh(mesh.devices.reshape(8, 4, 4, 2), ("z", "x", "row", "col"))
    whole = ("z", "x", "col")
    placed = (P(whole, "row"), P("row", whole), P(whole, "row"), P(whole, "row"))
    return jax.shard_map(
        on_device,
        mesh=mesh,
        in_specs=placed,
        out_specs=(P(whole, "row"), P(whole, "row"), P("row", whole), P(whole, "row")),
        check_vma=False,
    )
```

```python
import jax
import jax.numpy as jnp
from jax import lax
from jax.experimental import pallas as pl
from jax.experimental.pallas import tpu as pltpu
from jax.sharding import Mesh, PartitionSpec as P

BF = jnp.bfloat16
F32 = jnp.float32
SIZE = {"z": 8, "x": 4, "row": 4, "col": 2}
ORDER = (0, 1, 7, 2, 6, 3, 5, 4)
HEAD = 5


def smooth_gate(value):
    return 0.5 * value * (1.0 + lax.erf(value * 0.7071067811865476))


def smooth_slope(value):
    cumul = 0.5 * (1.0 + lax.erf(value * 0.7071067811865476))
    return cumul + value * jnp.exp(-0.5 * value * value) * 0.3989422804014327


def send(value, axis, shift):
    size = SIZE[axis]
    return lax.ppermute(value, axis, [(i, (i + shift) % size) for i in range(size)])


def token_pair(value):
    return lax.ppermute(value, "x", [(0, 1), (1, 0), (2, 3), (3, 2)])


def weight_pair(value):
    return lax.ppermute(value, "x", [(0, 3), (3, 0), (1, 2), (2, 1)])


def after(value, other):
    return lax.optimization_barrier((value, other))[0]


def call(body, outs, args, flops=1 << 20, scratch=()):
    specs = [pl.BlockSpec(memory_space=pltpu.SMEM)]
    specs += [pl.BlockSpec(memory_space=pltpu.VMEM)] * (len(args) - 1)
    kernel = pl.pallas_call(
        body,
        out_shape=outs,
        in_specs=specs,
        out_specs=[pl.BlockSpec(memory_space=pltpu.VMEM)] * len(outs),
        scratch_shapes=list(scratch),
        compiler_params=pltpu.CompilerParams(vmem_limit_bytes=40 << 20),
        cost_estimate=pl.CostEstimate(
            flops=flops, bytes_accessed=1 << 20, transcendentals=0
        ),
    )
    return list(kernel(*args))


def cat(values):
    return jnp.concatenate(values, 0)


def dot(a, b, dim_a, dim_b):
    return lax.dot_general(
        a, b, (((dim_a,), (dim_b,)), ((), ())), preferred_element_type=F32
    )


def products(value_of, weights, part):
    for s in range(2):
        part[s] = dot(weights[s], value_of(s), 1, 1).astype(part.dtype)


def quarter_of(tok, cot, index):
    rows = pl.ds(pl.multiple_of(index % 4 * 128, 128), 128)
    return lambda s: (tok, cot)[s][rows]


def up_kernel(me, *refs):
    held, (wi, wo, w_pair, tok, cot, weights), parts = refs[:8], refs[8:14], refs[14:]
    h = wi.shape[0]
    for s, w in enumerate((wi, wo)):
        weights[s, :h] = w[...]
        weights[s, h:] = w_pair[s * h : s * h + h]
    for q in range(4):
        half, chip = q // 2 * 4, q % 2
        for j in range(8):
            if j < 3:
                ref, i = held[half], j * 64 + chip * 32
            elif j < HEAD:
                ref, i = held[half + 1], chip * 64 + (j - 3) * 32
            else:
                ref, i = held[half + 2 + chip], (j - HEAD) * 32
            row = q * 128 + j * 16
            tok[row : row + 16] = ref[i : i + 16]
            cot[row : row + 16] = ref[i + 16 : i + 32]
    for k, part in zip((2, 1, 3), parts):
        products(quarter_of(tok, cot, me[0] + k), weights, part)


def mine_kernel(me, tok, cot, weights, part):
    products(quarter_of(tok, cot, me[0]), weights, part)


def act_kernel(me, p0, p1, p2, p3, out):
    del me
    pre, grad_act = p0[0], p0[1]
    for part in (p1, p2, p3):
        pre += part[0].astype(F32)
        grad_act += part[1].astype(F32)
    out[0] = smooth_gate(pre).astype(BF)
    out[1] = (grad_act * smooth_slope(pre)).astype(BF)


def down_kernel(me, c0, c2, c1, c3, weights, near, far, head, tail, full):
    for k, block in ((0, c0), (2, c2), (1, c1), (3, c3)):
        lane = pl.multiple_of(((me[0] + k) % 4) * 128, 128)
        full[:, :, pl.ds(lane, 128)] = block[...]
    for s in range(2):
        value = dot(full[s], weights[1 - s], 0, 0)
        for q in range(4):
            for j in range(8):
                piece = value[q * 128 + j * 16 : q * 128 + j * 16 + 16]
                row = j * 32 + s * 16
                if q < 2:
                    (near, far)[q][row : row + 16] = piece
                elif j < HEAD:
                    row += (4 - q) * HEAD * 32 - (2 * HEAD - 8) * 32
                    head[row : row + 16] = piece.astype(BF)
                else:
                    row -= HEAD * 32
                    (head, tail)[q - 2][row : row + 16] = piece.astype(BF)


def pair_kernel(me, full, tok, cot, out):
    del me
    h = full.shape[1] // 2
    out[:h] = dot(full[0, h:], cot[...], 1, 0).astype(BF)
    out[h:] = dot(full[1, h:], tok[...], 1, 0).astype(BF)


def own_kernel(me, full, tok, cot, grad_out, grad_in):
    del me
    h = full.shape[1] // 2
    grad_out[...] = dot(full[0, :h], cot[...], 1, 0)
    grad_in[...] = dot(full[1, :h], tok[...], 1, 0)


def on_device(tokens, w_in, w_out, cotangent):
    me = lax.axis_index("row").astype(jnp.int32).reshape(1)
    d, h = w_in.shape
    shape = jax.ShapeDtypeStruct
    flops = 2 * 1024 * d * h

    base = cat([tokens, cotangent])
    z = {2: send(base, "z", -2), 6: send(base, "z", 2)}
    both = cat([base, token_pair(base)])
    w_in_t = w_in.T
    w_pair = weight_pair(after(cat([w_in_t, w_out]), base))
    z[3], z[5] = send(z[2], "z", -1), send(z[6], "z", 1)
    second = cat([z[2], z[6]])
    z[4] = send(after(z[6], second), "z", 2)
    second = cat([second, token_pair(second)])
    near_t = cat([z[k] for k in ORDER[HEAD:]])
    both = after(both, z[3])
    first = cat([both, send(both, "z", -1), send(both, "z", 1)])
    far_t = after(token_pair(near_t), w_pair)
    held = [first, second, near_t, far_t]
    held += [send(value, "col", 1) for value in held]

    part, rounded = shape((2, 2 * h, 128), F32), shape((2, 2 * h, 128), BF)
    tok, cot, weights, *parts = call(
        up_kernel,
        [shape((512, d), BF)] * 2 + [shape((2, 2 * h, d), BF)] + [rounded] * 3,
        [me, *held, w_in_t, w_out, w_pair],
        flops,
    )
    mine = call(mine_kernel, [part], [me, after(tok, parts[0]), cot, weights], flops)
    parts[1:] = after(tuple(parts[1:]), mine[0])
    parts = mine + [send(value, "row", k) for k, value in zip((2, 1, 3), parts)]
    (block,) = call(act_kernel, [rounded], [me, *parts])
    blocks = [block] + [send(block, "row", -k) for k in (2, 1, 3)]

    sums = shape((256, d), F32)
    near, far, head, tail, full = call(
        down_kernel,
        [sums, sums, shape((256 + HEAD * 32, d), BF), shape((256 - HEAD * 32, d), BF), shape((2, 2 * h, 512), BF)],
        [me, *blocks, weights],
        2 * flops,
    )
    cut, rest = HEAD * 32, (8 - HEAD) * 32
    tail = send(tail, "col", 1)
    head = send(after(head, tail), "col", 1).astype(F32)
    far_t = (far[cut:] + tail.astype(F32)).astype(BF)
    far = after(far, far_t)
    (pair,) = call(
        pair_kernel, [shape((2 * h, d), BF)], [me, after(full, far_t), tok, cot], flops
    )
    pair = weight_pair(pair)
    grad_out, grad_in_t = call(
        own_kernel, [shape((h, d), F32)] * 2, [me, full, after(tok, far_t), cot], flops
    )
    head = after(head, grad_out)
    far_h = far[:cut] + head[rest:256]
    near_h = near[:cut] + head[256:]
    up_1 = cat([near_h[32:64], far_h[32:64]]).astype(BF)
    down_1 = cat([near_h[64:96], far_h[64:96]]).astype(BF)
    near, head = after((near, head), (up_1, down_1))
    up_1, down_1 = send(up_1, "z", 1).astype(F32), send(down_1, "z", -1).astype(F32)
    far_2 = far_h[96:].astype(BF)
    far_t = after(token_pair(far_t), far_2)
    far_2 = token_pair(far_2).astype(F32)
    third = (near[cut:] + head[:rest] + far_t.astype(F32)).astype(BF)
    up_2 = send(third[64:], "z", 2)
    up, down = send(third[:32], "z", 1), send(third[32:64], "z", -1)
    far_0 = after(far_h[:32], third) + up_1[32:] + down_1[32:]
    far_0 = token_pair(far_0.astype(BF)).astype(F32)
    near_2 = after(near_h[96:], far_0)
    up = (up_2.astype(F32) + up.astype(F32) + near_2[:32] + far_2[:32]).astype(BF)
    down = (down.astype(F32) + near_2[32:] + far_2[32:]).astype(BF)
    total = after(near_h[:32], up) + up_1[:32] + down_1[:32] + far_0
    total += send(up, "z", 2).astype(F32) + send(down, "z", -2).astype(F32)
    output, input_grad = total[:16].astype(BF), total[16:].astype(BF)
    grad_out = grad_out + pair[:h].astype(F32)
    grad_in_t = grad_in_t + pair[h:].astype(F32)
    return (output, input_grad, grad_in_t.T, grad_out)


def solution(mesh):
    mesh = Mesh(mesh.devices.reshape(8, 4, 4, 2), ("z", "x", "row", "col"))
    whole = ("z", "x", "col")
    placed = (P(whole, "row"), P("row", whole), P(whole, "row"), P(whole, "row"))
    return jax.shard_map(
        on_device,
        mesh=mesh,
        in_specs=placed,
        out_specs=(P(whole, "row"), P(whole, "row"), P("row", whole), P(whole, "row")),
        check_vma=False,
    )
```

```python
import jax
import jax.numpy as jnp
from jax import lax
from jax.experimental import pallas as pl
from jax.experimental.pallas import tpu as pltpu
from jax.sharding import Mesh, PartitionSpec as P

BF = jnp.bfloat16
F32 = jnp.float32
SIZE = {"z": 8, "x": 4, "row": 4, "col": 2}
ORDER = (0, 1, 7, 2, 6, 3, 5, 4)
HEAD = 5


def smooth_gate(value):
    return 0.5 * value * (1.0 + lax.erf(value * 0.7071067811865476))


def smooth_slope(value):
    cumul = 0.5 * (1.0 + lax.erf(value * 0.7071067811865476))
    return cumul + value * jnp.exp(-0.5 * value * value) * 0.3989422804014327


def send(value, axis, shift):
    size = SIZE[axis]
    return lax.ppermute(value, axis, [(i, (i + shift) % size) for i in range(size)])


def token_pair(value):
    return lax.ppermute(value, "x", [(0, 1), (1, 0), (2, 3), (3, 2)])


def weight_pair(value):
    return lax.ppermute(value, "x", [(0, 3), (3, 0), (1, 2), (2, 1)])


def after(value, other):
    return lax.optimization_barrier((value, other))[0]


def call(body, outs, args, flops=1 << 20, scratch=()):
    specs = [pl.BlockSpec(memory_space=pltpu.SMEM)]
    specs += [pl.BlockSpec(memory_space=pltpu.VMEM)] * (len(args) - 1)
    kernel = pl.pallas_call(
        body,
        out_shape=outs,
        in_specs=specs,
        out_specs=[pl.BlockSpec(memory_space=pltpu.VMEM)] * len(outs),
        scratch_shapes=list(scratch),
        compiler_params=pltpu.CompilerParams(vmem_limit_bytes=40 << 20),
        cost_estimate=pl.CostEstimate(
            flops=flops, bytes_accessed=1 << 20, transcendentals=0
        ),
    )
    return list(kernel(*args))


def cat(values):
    return jnp.concatenate(values, 0)


def dot(a, b, dim_a, dim_b):
    return lax.dot_general(
        a, b, (((dim_a,), (dim_b,)), ((), ())), preferred_element_type=F32
    )


def products(value_of, weights, part):
    for s in range(2):
        part[s] = dot(weights[s], value_of(s), 1, 1).astype(part.dtype)


def quarter_of(tok, cot, index):
    rows = pl.ds(pl.multiple_of(index % 4 * 128, 128), 128)
    return lambda s: (tok, cot)[s][rows]


def up_kernel(me, *refs):
    held, (wi, wo, w_pair, tok, cot, weights), parts = refs[:8], refs[8:14], refs[14:]
    h = wi.shape[0]
    for s, w in enumerate((wi, wo)):
        weights[s, :h] = w[...]
        weights[s, h:] = w_pair[s * h : s * h + h]
    for q in range(4):
        half, chip = q // 2 * 4, q % 2
        for j in range(8):
            if j < 3:
                ref, i = held[half], j * 64 + chip * 32
            elif j < HEAD:
                ref, i = held[half + 1], chip * 64 + (j - 3) * 32
            else:
                ref, i = held[half + 2 + chip], (j - HEAD) * 32
            row = q * 128 + j * 16
            tok[row : row + 16] = ref[i : i + 16]
            cot[row : row + 16] = ref[i + 16 : i + 32]
    for k, part in zip((2, 1, 3), parts):
        products(quarter_of(tok, cot, me[0] + k), weights, part)


def mine_kernel(me, tok, cot, weights, part):
    products(quarter_of(tok, cot, me[0]), weights, part)


def act_kernel(me, p0, p1, p2, p3, out):
    del me
    pre, grad_act = p0[0], p0[1]
    for part in (p1, p2, p3):
        pre += part[0].astype(F32)
        grad_act += part[1].astype(F32)
    out[0] = smooth_gate(pre).astype(BF)
    out[1] = (grad_act * smooth_slope(pre)).astype(BF)


def down_kernel(me, c0, c2, c1, c3, weights, near, far, head, tail, full):
    for k, block in ((0, c0), (2, c2), (1, c1), (3, c3)):
        lane = pl.multiple_of(((me[0] + k) % 4) * 128, 128)
        full[:, :, pl.ds(lane, 128)] = block[...]
    for s in range(2):
        value = dot(full[s], weights[1 - s], 0, 0)
        for q in range(4):
            for j in range(8):
                piece = value[q * 128 + j * 16 : q * 128 + j * 16 + 16]
                row = j * 32 + s * 16
                if q < 2:
                    (near, far)[q][row : row + 16] = piece
                elif j < HEAD:
                    row += (4 - q) * HEAD * 32 - (2 * HEAD - 8) * 32
                    head[row : row + 16] = piece.astype(BF)
                else:
                    row -= HEAD * 32
                    (head, tail)[q - 2][row : row + 16] = piece.astype(BF)


def pair_kernel(me, full, tok, cot, out):
    del me
    h = full.shape[1] // 2
    out[:h] = dot(full[0, h:], cot[...], 1, 0).astype(BF)
    out[h:] = dot(full[1, h:], tok[...], 1, 0).astype(BF)


def own_kernel(me, full, tok, cot, grad_out, grad_in):
    del me
    h = full.shape[1] // 2
    grad_out[...] = dot(full[0, :h], cot[...], 1, 0)
    grad_in[...] = dot(full[1, :h], tok[...], 1, 0)


def on_device(tokens, w_in, w_out, cotangent):
    me = lax.axis_index("row").astype(jnp.int32).reshape(1)
    d, h = w_in.shape
    shape = jax.ShapeDtypeStruct
    flops = 2 * 1024 * d * h

    top = lax.broadcasted_iota(jnp.int32, (32, d), 0) < 16
    base = jnp.where(
        top, jnp.pad(tokens, ((0, 16), (0, 0))), jnp.pad(cotangent, ((16, 0), (0, 0)))
    )
    z = {2: send(base, "z", -2), 6: send(base, "z", 2)}
    both = cat([base, token_pair(base)])
    w_in_t = w_in.T
    w_pair = weight_pair(after(cat([w_in_t, w_out]), base))
    z[3], z[5] = send(z[2], "z", -1), send(z[6], "z", 1)
    second = cat([z[2], z[6]])
    z[4] = send(after(z[6], second), "z", 2)
    second = cat([second, token_pair(second)])
    near_t = cat([z[k] for k in ORDER[HEAD:]])
    both = after(both, z[3])
    first = cat([both, send(both, "z", -1), send(both, "z", 1)])
    far_t = after(token_pair(near_t), w_pair)
    held = [first, second, near_t, far_t]
    held += [send(value, "col", 1) for value in held]

    part, rounded = shape((2, 2 * h, 128), F32), shape((2, 2 * h, 128), BF)
    tok, cot, weights, *parts = call(
        up_kernel,
        [shape((512, d), BF)] * 2 + [shape((2, 2 * h, d), BF)] + [rounded] * 3,
        [me, *held, w_in_t, w_out, w_pair],
        flops,
    )
    mine = call(mine_kernel, [part], [me, after(tok, parts[0]), cot, weights], flops)
    parts[1:] = after(tuple(parts[1:]), mine[0])
    parts = mine + [send(value, "row", k) for k, value in zip((2, 1, 3), parts)]
    (block,) = call(act_kernel, [rounded], [me, *parts])
    blocks = [block] + [send(block, "row", -k) for k in (2, 1, 3)]

    sums = shape((256, d), F32)
    near, far, head, tail, full = call(
        down_kernel,
        [sums, sums, shape((256 + HEAD * 32, d), BF), shape((256 - HEAD * 32, d), BF), shape((2, 2 * h, 512), BF)],
        [me, *blocks, weights],
        2 * flops,
    )
    cut, rest = HEAD * 32, (8 - HEAD) * 32
    tail = send(tail, "col", 1)
    head = send(after(head, tail), "col", 1).astype(F32)
    far_t = (far[cut:] + tail.astype(F32)).astype(BF)
    far = after(far, far_t)
    (pair,) = call(
        pair_kernel, [shape((2 * h, d), BF)], [me, after(full, far_t), tok, cot], flops
    )
    pair = weight_pair(pair)
    grad_out, grad_in_t = call(
        own_kernel, [shape((h, d), F32)] * 2, [me, full, after(tok, far_t), cot], flops
    )
    head = after(head, grad_out)
    far_h = far[:cut] + head[rest:256]
    near_h = near[:cut] + head[256:]
    up_1 = cat([near_h[32:64], far_h[32:64]]).astype(BF)
    down_1 = cat([near_h[64:96], far_h[64:96]]).astype(BF)
    near, head = after((near, head), (up_1, down_1))
    up_1, down_1 = send(up_1, "z", 1).astype(F32), send(down_1, "z", -1).astype(F32)
    far_2 = far_h[96:].astype(BF)
    far_t = after(token_pair(far_t), far_2)
    far_2 = token_pair(far_2).astype(F32)
    third = (near[cut:] + head[:rest] + far_t.astype(F32)).astype(BF)
    up_2 = send(third[64:], "z", 2)
    up, down = send(third[:32], "z", 1), send(third[32:64], "z", -1)
    far_0 = after(far_h[:32], third) + up_1[32:] + down_1[32:]
    far_0 = token_pair(far_0.astype(BF)).astype(F32)
    near_2 = after(near_h[96:], far_0)
    up = (up_2.astype(F32) + up.astype(F32) + near_2[:32] + far_2[:32]).astype(BF)
    down = (down.astype(F32) + near_2[32:] + far_2[32:]).astype(BF)
    total = after(near_h[:32], up) + up_1[:32] + down_1[:32] + far_0
    total += send(up, "z", 2).astype(F32) + send(down, "z", -2).astype(F32)
    output, input_grad = total[:16].astype(BF), total[16:].astype(BF)
    grad_out = grad_out + pair[:h].astype(F32)
    grad_in_t = grad_in_t + pair[h:].astype(F32)
    return (output, input_grad, grad_in_t.T, grad_out)


def solution(mesh):
    mesh = Mesh(mesh.devices.reshape(8, 4, 4, 2), ("z", "x", "row", "col"))
    whole = ("z", "x", "col")
    placed = (P(whole, "row"), P("row", whole), P(whole, "row"), P(whole, "row"))
    return jax.shard_map(
        on_device,
        mesh=mesh,
        in_specs=placed,
        out_specs=(P(whole, "row"), P(whole, "row"), P("row", whole), P(whole, "row")),
        check_vma=False,
    )
```

```python
import jax
import jax.numpy as jnp
from jax import lax
from jax.experimental import pallas as pl
from jax.experimental.pallas import tpu as pltpu
from jax.sharding import Mesh, PartitionSpec as P

BF = jnp.bfloat16
F32 = jnp.float32
SIZE = {"z": 8, "x": 4, "row": 4, "col": 2}
ORDER = (0, 1, 7, 2, 6, 3, 5, 4)
HEAD = 5


def smooth_gate(value):
    return 0.5 * value * (1.0 + lax.erf(value * 0.7071067811865476))


def smooth_slope(value):
    cumul = 0.5 * (1.0 + lax.erf(value * 0.7071067811865476))
    return cumul + value * jnp.exp(-0.5 * value * value) * 0.3989422804014327


def send(value, axis, shift):
    size = SIZE[axis]
    return lax.ppermute(value, axis, [(i, (i + shift) % size) for i in range(size)])


def token_pair(value):
    return lax.ppermute(value, "x", [(0, 1), (1, 0), (2, 3), (3, 2)])


def weight_pair(value):
    return lax.ppermute(value, "x", [(0, 3), (3, 0), (1, 2), (2, 1)])


def after(value, other):
    return lax.optimization_barrier((value, other))[0]


def call(body, outs, args, flops=1 << 20, scratch=()):
    specs = [pl.BlockSpec(memory_space=pltpu.SMEM)]
    specs += [pl.BlockSpec(memory_space=pltpu.VMEM)] * (len(args) - 1)
    kernel = pl.pallas_call(
        body,
        out_shape=outs,
        in_specs=specs,
        out_specs=[pl.BlockSpec(memory_space=pltpu.VMEM)] * len(outs),
        scratch_shapes=list(scratch),
        compiler_params=pltpu.CompilerParams(vmem_limit_bytes=40 << 20),
        cost_estimate=pl.CostEstimate(
            flops=flops, bytes_accessed=1 << 20, transcendentals=0
        ),
    )
    return list(kernel(*args))


def cat(values):
    return jnp.concatenate(values, 0)


def dot(a, b, dim_a, dim_b):
    return lax.dot_general(
        a, b, (((dim_a,), (dim_b,)), ((), ())), preferred_element_type=F32
    )


def products(value_of, wi, wo, w_pair, part):
    h = wi.shape[0]
    for s, w in enumerate((wi, wo)):
        part[s, :h] = dot(w[...], value_of(s), 1, 1).astype(part.dtype)
        part[s, h:] = dot(w_pair[s * h : s * h + h], value_of(s), 1, 1).astype(part.dtype)


def quarter_of(tok, cot, index):
    rows = pl.ds(pl.multiple_of(index % 4 * 128, 128), 128)
    return lambda s: (tok, cot)[s][rows]


def up_kernel(me, *refs):
    held, (wi, wo, w_pair, tok, cot), parts = refs[:8], refs[8:13], refs[13:]
    for q in range(4):
        half, chip = q // 2 * 4, q % 2
        for j in range(8):
            if j < 3:
                ref, i = held[half], j * 64 + chip * 32
            elif j < HEAD:
                ref, i = held[half + 1], chip * 64 + (j - 3) * 32
            else:
                ref, i = held[half + 2 + chip], (j - HEAD) * 32
            row = q * 128 + j * 16
            tok[row : row + 16] = ref[i : i + 16]
            cot[row : row + 16] = ref[i + 16 : i + 32]
    for k, part in zip((2, 1, 3), parts):
        products(quarter_of(tok, cot, me[0] + k), wi, wo, w_pair, part)


def mine_kernel(me, tok, cot, wi, wo, w_pair, part):
    products(quarter_of(tok, cot, me[0]), wi, wo, w_pair, part)


def act_kernel(me, p0, p1, p2, p3, out):
    del me
    pre, grad_act = p0[0], p0[1]
    for part in (p1, p2, p3):
        pre += part[0].astype(F32)
        grad_act += part[1].astype(F32)
    out[0] = smooth_gate(pre).astype(BF)
    out[1] = (grad_act * smooth_slope(pre)).astype(BF)


def down_kernel(me, full, wi, wo, w_pair, near, far, head, tail):
    del me
    h = wi.shape[0]
    for s, w in enumerate((wo, wi)):
        value = dot(full[s, :h], w[...], 0, 0)
        value += dot(full[s, h:], w_pair[(1 - s) * h : (2 - s) * h], 0, 0)
        for q in range(4):
            for j in range(8):
                piece = value[q * 128 + j * 16 : q * 128 + j * 16 + 16]
                row = j * 32 + s * 16
                if q < 2:
                    (near, far)[q][row : row + 16] = piece
                elif j < HEAD:
                    row += (3 - q) * HEAD * 32
                    head[row : row + 16] = piece.astype(BF)
                else:
                    row += (3 - q) * (8 - HEAD) * 32 - HEAD * 32
                    tail[row : row + 16] = piece.astype(BF)


def pair_kernel(me, b0, b2, b1, b3, tok, cot, full, out):
    h = full.shape[1] // 2
    for k, block in ((0, b0), (2, b2), (1, b1), (3, b3)):
        lane = pl.multiple_of(((me[0] + k) % 4) * 128, 128)
        full[:, :, pl.ds(lane, 128)] = block[...]
    out[:h] = dot(full[0, h:], cot[...], 1, 0).astype(BF)
    out[h:] = dot(full[1, h:], tok[...], 1, 0).astype(BF)


def own_kernel(me, full, tok, cot, grad_out, grad_in):
    del me
    h = full.shape[1] // 2
    grad_out[...] = dot(full[0, :h], cot[...], 1, 0)
    grad_in[...] = dot(full[1, :h], tok[...], 1, 0)


def on_device(tokens, w_in, w_out, cotangent):
    me = lax.axis_index("row").astype(jnp.int32).reshape(1)
    d, h = w_in.shape
    shape = jax.ShapeDtypeStruct
    flops = 2 * 1024 * d * h

    top = lax.broadcasted_iota(jnp.int32, (32, d), 0) < 16
    base = jnp.where(
        top, jnp.pad(tokens, ((0, 16), (0, 0))), jnp.pad(cotangent, ((16, 0), (0, 0)))
    )
    z = {2: send(base, "z", -2), 6: send(base, "z", 2)}
    both = cat([base, token_pair(base)])
    w_in_t = w_in.T
    w_pair = weight_pair(after(cat([w_in_t, w_out]), base))
    z[3], z[5] = send(z[2], "z", -1), send(z[6], "z", 1)
    second = cat([z[2], z[6]])
    z[4] = send(after(z[6], second), "z", 2)
    second = cat([second, token_pair(second)])
    near_t = cat([z[k] for k in ORDER[HEAD:]])
    both = after(both, z[3])
    first = cat([both, send(both, "z", -1), send(both, "z", 1)])
    far_t = after(token_pair(near_t), w_pair)
    held = [first, second, near_t, far_t]
    held += [send(value, "col", 1) for value in held]

    part, rounded = shape((2, 2 * h, 128), F32), shape((2, 2 * h, 128), BF)
    weights = [w_in_t, w_out, w_pair]
    tok, cot, *parts = call(
        up_kernel, [shape((512, d), BF)] * 2 + [rounded] * 3, [me, *held, *weights], flops
    )
    mine = call(mine_kernel, [part], [me, after(tok, parts[0]), cot, *weights], flops)
    parts = mine + [send(value, "row", k) for k, value in zip((2, 1, 3), parts)]
    (block,) = call(act_kernel, [rounded], [me, *parts])
    blocks = [block] + [send(block, "row", -k) for k in (2, 1, 3)]

    sums = shape((256, d), F32)
    full, pair = call(
        pair_kernel,
        [shape((2, 2 * h, 512), BF), shape((2 * h, d), BF)],
        [me, *blocks, tok, cot],
        flops,
    )
    near, far, head, tail = call(
        down_kernel,
        [sums, sums, shape((HEAD * 64, d), BF), shape(((8 - HEAD) * 64, d), BF)],
        [me, full, w_in_t, w_out, w_pair],
        2 * flops,
    )
    cut, rest = HEAD * 32, (8 - HEAD) * 32
    tail = send(tail, "col", 1)
    head = send(after(head, tail), "col", 1).astype(F32)
    tail = tail.astype(F32)
    far_t = (far[cut:] + tail[:rest]).astype(BF)
    far = after(far, far_t)
    pair = weight_pair(after(pair, far_t))
    grad_out, grad_in_t = call(
        own_kernel, [shape((h, d), F32)] * 2, [me, full, after(tok, far_t), cot], flops
    )
    far_t = token_pair(far_t)
    head = after(head, grad_out)
    far_h = far[:cut] + head[:cut]
    near_h = near[:cut] + head[cut:]
    up_1 = cat([near_h[32:64], far_h[32:64]]).astype(BF)
    down_1 = cat([near_h[64:96], far_h[64:96]]).astype(BF)
    near = after(near, (up_1, down_1))
    up_1, down_1 = send(up_1, "z", 1).astype(F32), send(down_1, "z", -1).astype(F32)
    far_2 = token_pair(far_h[96:].astype(BF)).astype(F32)
    third = (near[cut:] + tail[rest:] + far_t.astype(F32)).astype(BF)
    up, down = send(third[:32], "z", 1), send(third[32:64], "z", -1)
    up_2 = send(third[64:], "z", 2)
    far_0 = after(far_h[:32], third) + up_1[32:] + down_1[32:]
    far_0 = token_pair(far_0.astype(BF)).astype(F32)
    near_2 = after(near_h[96:], far_0)
    up = (up.astype(F32) + up_2.astype(F32) + near_2[:32] + far_2[:32]).astype(BF)
    down = (down.astype(F32) + near_2[32:] + far_2[32:]).astype(BF)
    total = after(near_h[:32], up) + up_1[:32] + down_1[:32] + far_0
    total += send(up, "z", 2).astype(F32) + send(down, "z", -2).astype(F32)
    output, input_grad = total[:16].astype(BF), total[16:].astype(BF)
    grad_out = grad_out + pair[:h].astype(F32)
    grad_in_t = grad_in_t + pair[h:].astype(F32)
    return (output, input_grad, grad_in_t.T, grad_out)


def solution(mesh):
    mesh = Mesh(mesh.devices.reshape(8, 4, 4, 2), ("z", "x", "row", "col"))
    whole = ("z", "x", "col")
    placed = (P(whole, "row"), P("row", whole), P(whole, "row"), P(whole, "row"))
    return jax.shard_map(
        on_device,
        mesh=mesh,
        in_specs=placed,
        out_specs=(P(whole, "row"), P(whole, "row"), P("row", whole), P(whole, "row")),
        check_vma=False,
    )
```
